32 devices in a mesh: rcv: 16 (over z, x, core), src: 2 (over y).
Axes of the slice: x: 2, y: 2, z: 4, core: 2. Of those that a mesh axis runs over, the one named last changes fastest.
Arguments:
- records: float32 [1024, 4096], P(('rcv', 'src')), may hold values from -6 to 6
- window_start: int32 [32], P(('rcv', 'src')), may hold values from 0 to 16
- channel_segment: int32 [1024], replicated, may hold values from 0 to 63, as said below
- segment_row: int32 [64], replicated, may hold values from 0 to 63, as said below
Outputs:
- stacks: float32 [64, 16, 256], P('rcv', 'src')
The draws below stay inside these ranges and needn't reach their ends.
Inputs may be any that keep to these rules, and one draw needn't show every extreme that they name: `window_start`: window positions index the group's 64 channels with the tile's own 32 channels left out. A permutation: segment s is stacked into row segment_row[s], held by rcv index segment_row[s] // 4. `channel_segment`: the 32 channels of each tile (aligned blocks) lie in segments of exactly 16 rcv indices, exactly 2 channels for each; one rcv index receives 2 channels from every tile.
All inputs are finite; a program needn't handle non-finite values.
Results may differ from the reference program's by a relative error of at most 0.0058.
Values may be sent and summed in bfloat16 or wider, within the bound.
A program may use at most 64 MiB of HBM per device.

```python
import math
import jax
import jax.numpy as jnp
from jax import lax

NFFT = 1024
LAGS = 256
NBLK = 4
CH_DEV = 32
CAP = 2
SEG_PER = 4
GRP = 64
NWIN = 16
TILES = 32
CHANNELS = 1024
NSEG = 64
SAMPLES = 4096
N_RCV = 16
N_SRC = 2


def routing_draw(key):
    base_key = jax.random.fold_in(key, 7)
    perm_key, bias_key, favored_key, noise_key, order_key, slot_key = jax.random.split(base_key, 6)
    segment_row = jax.random.permutation(perm_key, NSEG).astype(jnp.int32)
    row_segment = jnp.argsort(segment_row).astype(jnp.int32)
    owner_ids = jnp.arange(N_RCV, dtype=jnp.int32)
    biases = jax.random.randint(bias_key, (N_RCV,), 0, 98304)
    favored = jax.random.randint(favored_key, (), 0, N_RCV)
    biases = jnp.where(owner_ids == favored, 262144, biases)
    noises = jax.random.randint(noise_key, (TILES, N_RCV), 0, 65536)
    scores = (noises + biases[None, :]) * N_RCV + owner_ids[None, :]
    chosen = lax.top_k(scores, CH_DEV // CAP)[1].astype(jnp.int32)
    owners = jnp.repeat(chosen, CAP, axis=1)
    order_scores = jax.random.randint(order_key, (TILES, CH_DEV), 0, 1048576) * CH_DEV + jnp.arange(CH_DEV, dtype=jnp.int32)[None, :]
    owners = jnp.take_along_axis(owners, jnp.argsort(order_scores, axis=1), axis=1)
    slots = jax.random.randint(slot_key, (TILES, CH_DEV), 0, SEG_PER)
    channel_segment = row_segment[(owners * SEG_PER + slots).reshape(-1)]
    return (segment_row, channel_segment.astype(jnp.int32))


def draw_channel_segment(key, part):
    return routing_draw(key)[1]


def draw_segment_row(key, part):
    return routing_draw(key)[0]


def with_ends(entries, key, low, top_value):
    longest = entries.shape.index(max(entries.shape))
    spots = []
    for shift in (0, 1):
        where = [jax.random.randint(jax.random.fold_in(key, axis), (), 0, length) for axis, length in enumerate(entries.shape)]
        where[longest] = (where[longest] + shift) % entries.shape[longest]
        spots.append(tuple(where))
    return entries.at[spots[0]].set(low).at[spots[1]].set(top_value)


def block_levels(key, dims, cuts, low, high):
    factor_of, own = 1.0, jax.random.fold_in(key, 6)
    for dim, shards_of in cuts:
        heights = jnp.exp(jax.random.uniform(jax.random.fold_in(own, dim), (shards_of,), jnp.float32, low / len(cuts), high / len(cuts)))
        factor_of = factor_of * jnp.repeat(heights, dims[dim] // shards_of).reshape([-1 if axis == dim else 1 for axis in range(len(dims))])
    return factor_of


def bell_draw(own_key, extent, spread, limit, cuts=(), kind=jnp.bfloat16):
    array = jax.random.normal(own_key, extent, jnp.float32) * spread
    if len(cuts) > 0:
        array = block_levels(own_key, extent, cuts, -0.22, 0.18) * array
    return jnp.clip(array, min=-limit, max=limit).astype(kind)


def setup_inputs(seed: int = 0) -> dict:
    key_list = jax.random.split(jax.random.key(seed), 5)
    return {
        "records": bell_draw(key_list[0], (CHANNELS, SAMPLES), 1.0, 6.0, ((0, 32),), jnp.float32),
        "window_start": with_ends(jax.random.randint(key_list[1], (TILES,), 0, GRP - CH_DEV - NWIN + 1), jax.random.fold_in(key_list[1], 1), 0, GRP - CH_DEV - NWIN).astype(jnp.int32),
        "channel_segment": draw_channel_segment(jax.random.fold_in(key_list[4], 71), 0),
        "segment_row": draw_segment_row(jax.random.fold_in(key_list[4], 71), 0),
    }


def dft_table(length):
    sample_index = jnp.arange(length, dtype=jnp.int32)
    frequency = jnp.arange(length // 2, dtype=jnp.int32)
    angles = (sample_index[:, None] * frequency[None, :] % length).astype(jnp.float32) * (2.0 * math.pi / length)
    return jnp.concatenate([jnp.cos(angles), -jnp.sin(angles)], axis=1)

def lag_table(length, lag_count):
    frequency = jnp.arange(length // 2, dtype=jnp.int32)
    shifts = jnp.arange(lag_count, dtype=jnp.int32) - lag_count // 2
    angles = (frequency[:, None] * shifts[None, :] % length).astype(jnp.float32) * (2.0 * math.pi / length)
    return jnp.concatenate([jnp.cos(angles), -jnp.sin(angles)], axis=0).astype(jnp.bfloat16)

def whiten(spectrum):
    half_size = spectrum.shape[-1] // 2
    powers = spectrum[..., :half_size] ** 2 + spectrum[..., half_size:] ** 2
    mean_power = lax.optimization_barrier(jnp.mean(powers, axis=-1, keepdims=True))
    magnitude = jnp.sqrt(powers + 0.1 * mean_power + 1e-06)
    return spectrum / jnp.concatenate([magnitude, magnitude], axis=-1)

def correlate(own_tile, sources, lag_rows, block_count):
    half_size = own_tile.shape[-1] // 2
    left_part = own_tile.astype(jnp.float32)
    right_part = sources.astype(jnp.float32)
    left_re, left_im = (left_part[..., :half_size], left_part[..., half_size:])
    right_re, right_im = (right_part[..., :half_size], right_part[..., half_size:])
    real_part = jnp.einsum('ibf,jbf->ijf', left_re, right_re) + jnp.einsum('ibf,jbf->ijf', left_im, right_im)
    imag_part = jnp.einsum('ibf,jbf->ijf', left_re, right_im) - jnp.einsum('ibf,jbf->ijf', left_im, right_re)
    cross_spec = jnp.concatenate([real_part, imag_part], axis=-1).astype(jnp.bfloat16)
    flat_rows = cross_spec.reshape(-1, cross_spec.shape[-1])
    correlation = jnp.dot(flat_rows, lag_rows, preferred_element_type=jnp.float32) / math.sqrt(block_count * half_size)
    return correlation.astype(jnp.bfloat16).reshape(own_tile.shape[0], sources.shape[0], lag_rows.shape[1])

def reference(records, window_start, channel_segment, segment_row):
    blocks = records.reshape(CHANNELS * NBLK, NFFT)
    spectrum = jnp.dot(blocks, dft_table(NFFT), precision=lax.Precision.HIGHEST, preferred_element_type=jnp.float32)
    white = whiten(spectrum).astype(jnp.bfloat16).reshape(CHANNELS, NBLK, NFFT)
    lag_rows = lag_table(NFFT, LAGS)
    stack_rows = segment_row[channel_segment]

    def tile_step(stacks, tile_index):
        group_first = tile_index // N_SRC * GRP
        position = tile_index % N_SRC
        own_tile = lax.dynamic_slice_in_dim(white, tile_index * CH_DEV, CH_DEV)
        window_idx = window_start[tile_index] + jnp.arange(NWIN, dtype=jnp.int32)
        source_idx = jnp.where(window_idx < position * CH_DEV, window_idx, window_idx + CH_DEV) + group_first
        sources = jnp.take(white, source_idx, axis=0)
        correlation = correlate(own_tile, sources, lag_rows, NBLK).astype(jnp.float32)
        tile_rows = lax.dynamic_slice_in_dim(stack_rows, tile_index * CH_DEV, CH_DEV)
        return (stacks.at[tile_rows].add(correlation), None)
    stacks = lax.scan(tile_step, jnp.zeros((NSEG, NWIN, LAGS), jnp.float32), jnp.arange(TILES, dtype=jnp.int32))[0]
    counts = jnp.zeros((NSEG,), jnp.float32).at[stack_rows].add(1.0)
    return stacks / jnp.sqrt(jnp.maximum(counts, 1.0))[:, None, None]
```

```python
import functools
import math

import jax
import jax.numpy as jnp
import ml_dtypes
import numpy as np
from jax import lax
from jax.experimental import pallas as pl
from jax.experimental.pallas import tpu as pltpu
from jax.sharding import PartitionSpec as P

NFFT = 1024
HALF = NFFT // 2
QUART = NFFT // 4
LAGS = 256
CAP = 2
SEG_PER = 4
LANES = 128
OWNERS_STEP = 4
MESH = pl.DeviceIdType.MESH
ORDER = np.concatenate([np.arange(r, HALF, 4) for r in (0, 2, 1, 3)])


def dft_tables():
    parts = []
    for r, rows in ((0, QUART), (2, QUART), (1, 2 * QUART), (3, 2 * QUART)):
        n = np.arange(rows)
        f = np.arange(r, HALF, 4)
        angles = (n[:, None] * f[None, :] % NFFT) * (2.0 * math.pi / NFFT)
        parts.append(np.concatenate([np.cos(angles), -np.sin(angles)], axis=1))
    table = np.concatenate(parts, axis=0).astype(np.float32)
    high = table.astype(ml_dtypes.bfloat16)
    low = (table - high.astype(np.float32)).astype(ml_dtypes.bfloat16)
    return np.stack([high, low])


def lag_table():
    shifts = np.arange(LAGS) - LAGS // 2
    angles = (ORDER[:, None] * shifts[None, :] % NFFT) * (2.0 * math.pi / NFFT)
    table = np.concatenate([np.cos(angles), -np.sin(angles)], axis=0)
    return table.astype(np.float32).astype(ml_dtypes.bfloat16)


def iota(shape, axis):
    return lax.broadcasted_iota(jnp.int32, shape, axis)


def onehot(mask):
    return jnp.where(mask, 1.0, 0.0).astype(jnp.bfloat16)


def mxu(a, b):
    return jnp.dot(a, b, preferred_element_type=jnp.float32)


def kernel(
    rcv_count,
    src_count,
    tile,
    blocks,
    window_start,
    segment_row,
    segments,
    records,
    tables,
    lag_rows,
    out,
    x,
    table,
    lags,
    owner_rows,
    starts_out,
    starts_in,
    white,
    sources_out,
    sources_in,
    own,
    sources,
    cross,
    buckets,
    arrived,
    load_sems,
    start_send,
    start_recv,
    source_send,
    source_recv,
    bucket_send,
    bucket_recv,
):
    rcv = lax.axis_index("rcv")
    pos = lax.axis_index("src")
    me = rcv * src_count + pos
    devices = rcv_count * src_count
    window = tile * src_count // 4
    part = window // src_count
    bucket_rows = rcv_count * CAP
    per_row = LANES // tile
    rows_dest = CAP * part

    loads = [
        pltpu.make_async_copy(records, x, load_sems.at[0]),
        pltpu.make_async_copy(tables, table, load_sems.at[1]),
        pltpu.make_async_copy(lag_rows, lags, load_sems.at[2]),
    ]
    for load in loads:
        load.start()

    barrier = pltpu.get_barrier_semaphore()

    def greet(step, carry):
        other = lax.rem(me + step, devices)
        pl.semaphore_signal(
            barrier,
            inc=1,
            device_id=(other // src_count, lax.rem(other, src_count)),
            device_id_type=MESH,
        )
        return carry

    lax.fori_loop(1, devices, greet, 0)

    starts_out[...] = jnp.full(starts_out.shape, window_start[0], jnp.int32)

    all_segments = segments[...]

    def look_up(segment, rows):
        return rows + jnp.where(all_segments == segment, segment_row[segment], 0)

    stack_rows = lax.fori_loop(
        0, segment_row.shape[0], look_up, jnp.zeros(all_segments.shape, jnp.int32), unroll=8
    )
    owners = stack_rows // SEG_PER
    slots = stack_rows - owners * SEG_PER
    owner_rows[...] = owners
    lane_a, lane_b = iota((LANES, LANES), 0), iota((LANES, LANES), 1)
    earlier = onehot((lane_a // tile == lane_b // tile) & (lane_a < lane_b))

    mine = owners == rcv
    ranks = mxu(onehot(mine), earlier)
    labels = jnp.zeros((owners.shape[0], LANES), jnp.float32)
    for rank in range(CAP):
        value = jnp.where(mine & (ranks == rank), slots + 1, 0).astype(jnp.bfloat16)
        spread = onehot(
            (lane_a // tile == lane_b // rows_dest % per_row) & (lane_b // part % CAP == rank)
        )
        labels = labels + mxu(value, spread)
    arrivals = devices * rows_dest
    labels = jnp.concatenate([labels] * (arrivals // LANES), axis=1)
    row_id = iota(labels.shape, 0)
    lane_id = iota(labels.shape, 1)
    labels = jnp.sum(
        jnp.where(row_id == lane_id // (rows_dest * per_row), labels, 0.0), axis=0, keepdims=True
    )
    out_id = iota((SEG_PER * part, arrivals), 0)
    lane_id = iota((SEG_PER * part, arrivals), 1)
    chosen = (labels == (out_id // part + 1).astype(jnp.float32)) & (
        out_id % part == lane_id % part
    )
    summing = jnp.where(chosen, 1.0, 0.0)
    counts = jnp.sum(summing, axis=1, keepdims=True)
    out_scale = 1.0 / jnp.sqrt(jnp.maximum(counts, 1.0))
    summing = summing.astype(jnp.bfloat16)

    tile_owners = owner_rows[pl.ds(me // per_row, 1), :]
    bucket_id = iota((bucket_rows, LANES), 0)
    held = bucket_id // CAP == tile_owners
    tile_ranks = mxu(onehot(held), earlier)
    placed = onehot(held & (tile_ranks == (bucket_id % CAP).astype(jnp.float32)))
    fold = onehot(
        (lane_a // tile == lax.rem(me, per_row)) & (lane_a % tile == lane_b % tile)
    )
    placed = mxu(placed, fold)
    placed = jnp.concatenate([placed] * blocks, axis=0)
    placed = jnp.where(
        iota(placed.shape, 0) // bucket_rows == iota(placed.shape, 1) // tile, placed, 0.0
    ).astype(jnp.bfloat16)

    pl.semaphore_wait(barrier, devices - 1)

    def start_copy(step):
        other = lax.rem(pos + step, src_count)
        return pltpu.make_async_remote_copy(
            src_ref=starts_out,
            dst_ref=starts_in.at[step - 1],
            send_sem=start_send.at[step - 1],
            recv_sem=start_recv.at[step - 1],
            device_id=(rcv, other),
            device_id_type=MESH,
        )

    for step in range(1, src_count):
        start_copy(step).start()

    loads[0].wait()
    quarters = []
    for quarter in range(4):
        quarters.append(
            jnp.concatenate(
                [
                    x[:, block * NFFT + quarter * QUART : block * NFFT + (quarter + 1) * QUART]
                    for block in range(blocks)
                ],
                axis=0,
            )
        )
    even_a, even_b = quarters[0] + quarters[2], quarters[1] + quarters[3]
    odd = jnp.concatenate([quarters[0] - quarters[2], quarters[1] - quarters[3]], axis=1)
    inputs = [even_a + even_b, even_a - even_b, odd, odd]
    loads[1].wait()
    height = blocks * tile
    real_parts, imag_parts = [], []
    first = 0
    for values in inputs:
        depth = values.shape[1]
        high = values.astype(jnp.bfloat16)
        low = (values - high.astype(jnp.float32)).astype(jnp.bfloat16)
        both = mxu(jnp.concatenate([high, low], axis=0), table[0, first : first + depth, :])
        total = both[:height] + both[height:] + mxu(high, table[1, first : first + depth, :])
        first += depth
        real_parts.append(total[:, :LANES])
        imag_parts.append(total[:, LANES:])
    real = jnp.concatenate(real_parts, axis=1)
    imag = jnp.concatenate(imag_parts, axis=1)
    powers = real * real + imag * imag
    mean_power = jnp.mean(powers, axis=1, keepdims=True)
    factor = lax.rsqrt(powers + 0.1 * mean_power + 1e-06)
    white[...] = jnp.concatenate([real * factor, imag * factor], axis=1).astype(jnp.bfloat16)

    def source_copy(step):
        other = lax.rem(pos + step, src_count)
        return pltpu.make_async_remote_copy(
            src_ref=sources_out.at[step - 1],
            dst_ref=sources_in.at[step - 1],
            send_sem=source_send.at[step - 1],
            recv_sem=source_recv.at[step - 1],
            device_id=(rcv, other),
            device_id_type=MESH,
        )

    for step in range(1, src_count):
        other = lax.rem(pos + step, src_count)
        start_copy(src_count - step).wait_recv()
        first_position = starts_in[src_count - step - 1, 0:1, :]
        my_place = pos - jnp.where(pos < other, 0, 1)
        row_id = iota((blocks * window, LANES), 0)
        lane_id = iota((blocks * window, LANES), 1)
        asked = (first_position + row_id % window == my_place * tile + lane_id % tile) & (
            row_id // window == lane_id // tile
        )
        sources_out[step - 1] = mxu(onehot(asked), white[...]).astype(jnp.bfloat16)
        source_copy(step).start()

    own[...] = mxu(placed, white[...])

    loads[2].wait()
    for step in range(1, src_count):
        source_copy(step).wait_recv()
    total = sources_in[0].astype(jnp.float32)
    for step in range(2, src_count):
        total = total + sources_in[step - 1].astype(jnp.float32)
    sources[...] = total

    scale = 1.0 / math.sqrt(blocks * HALF)
    steps = rcv_count // OWNERS_STEP
    group_rows = src_count * rows_dest

    def bucket_copy(owner, place):
        return pltpu.make_async_remote_copy(
            src_ref=buckets.at[owner * src_count + place],
            dst_ref=arrived.at[me],
            send_sem=bucket_send,
            recv_sem=bucket_recv,
            device_id=(owner, place),
            device_id_type=MESH,
        )

    def owner_step(step, carry):
        chunk = lax.rem(rcv // OWNERS_STEP + 1 + step, steps)

        def cross_step(index, inner):
            re_cols = pl.ds(pl.multiple_of(index * LANES, LANES), LANES)
            im_cols = pl.ds(pl.multiple_of(HALF + index * LANES, LANES), LANES)
            group = OWNERS_STEP * CAP
            left = []
            for block in range(blocks):
                first_row = pl.multiple_of(block * bucket_rows + chunk * group, group)
                rows = pl.ds(first_row, group)
                left.append((own[rows, re_cols], own[rows, im_cols]))
            for place in range(src_count):
                right = []
                for block in range(blocks):
                    rows = slice(block * window + place * part, block * window + (place + 1) * part)
                    right.append((sources[rows, re_cols], sources[rows, im_cols]))
                for owner in range(OWNERS_STEP):
                    reals, imags = [], []
                    for rank in range(CAP):
                        row = slice(owner * CAP + rank, owner * CAP + rank + 1)
                        re_sum, im_sum = None, None
                        for block in range(blocks):
                            left_re, left_im = left[block][0][row], left[block][1][row]
                            right_re, right_im = right[block]
                            re_term = left_re * right_re + left_im * right_im
                            im_term = left_re * right_im - left_im * right_re
                            re_sum = re_term if re_sum is None else re_sum + re_term
                            im_sum = im_term if im_sum is None else im_sum + im_term
                        reals.append(re_sum)
                        imags.append(im_sum)
                    at = owner * group_rows + place * rows_dest
                    rows = slice(at, at + rows_dest)
                    cross[rows, re_cols] = jnp.concatenate(reals, axis=0).astype(jnp.bfloat16)
                    cross[rows, im_cols] = jnp.concatenate(imags, axis=0).astype(jnp.bfloat16)
            return inner

        lax.fori_loop(0, HALF // LANES, cross_step, 0)
        rows = (mxu(cross[...], lags[...]) * scale).astype(jnp.bfloat16)
        dests = OWNERS_STEP * src_count
        buckets[pl.ds(chunk * dests, dests)] = rows.reshape(dests, rows_dest, LAGS)

        def send(index, inner):
            dest = chunk * dests + index

            @pl.when(dest != me)
            def _():
                bucket_copy(dest // src_count, lax.rem(dest, src_count)).start()

            return inner

        lax.fori_loop(0, dests, send, 0)
        return carry

    lax.fori_loop(0, steps, owner_step, 0)
    arrived[pl.ds(me, 1)] = buckets[pl.ds(me, 1)]

    others = pl.ds(0, devices - 1)
    pltpu.make_async_copy(arrived.at[others], arrived.at[others], bucket_recv).wait()
    stacked = mxu(summing, arrived[...].reshape(arrivals, LAGS)) * out_scale
    out[...] = stacked.reshape(SEG_PER, part, LAGS)

    pltpu.make_async_copy(buckets.at[others], buckets.at[others], bucket_send).wait()
    for step in range(1, src_count):
        start_copy(step).wait_send()
        source_copy(step).wait_send()


def on_device(rcv_count, src_count, records, window_start, channel_segment, segment_row):
    tile, samples = records.shape
    blocks = samples // NFFT
    devices = rcv_count * src_count
    window = tile * src_count // 4
    part = window // src_count
    rows_dest = CAP * part
    bucket_rows = rcv_count * CAP
    segments = channel_segment.reshape(-1, LANES)
    tables = jnp.asarray(dft_tables())
    lag_rows = jnp.asarray(lag_table())
    smem = pl.BlockSpec(memory_space=pltpu.SMEM)
    vmem = pl.BlockSpec(memory_space=pltpu.VMEM)
    anywhere = pl.BlockSpec(memory_space=pl.ANY)
    bf16, f32, i32 = jnp.bfloat16, jnp.float32, jnp.int32
    dma = pltpu.SemaphoreType.DMA
    return pl.pallas_call(
        functools.partial(kernel, rcv_count, src_count, tile, blocks),
        out_shape=jax.ShapeDtypeStruct((SEG_PER, part, LAGS), f32),
        in_specs=[smem, smem, vmem, anywhere, anywhere, anywhere],
        out_specs=vmem,
        scratch_shapes=[
            pltpu.VMEM(records.shape, f32),
            pltpu.VMEM(tables.shape, bf16),
            pltpu.VMEM(lag_rows.shape, bf16),
            pltpu.VMEM(segments.shape, i32),
            pltpu.VMEM((8, LANES), i32),
            pltpu.VMEM((src_count - 1, 8, LANES), i32),
            pltpu.VMEM((blocks * tile, NFFT), bf16),
            pltpu.VMEM((src_count - 1, blocks * window, NFFT), bf16),
            pltpu.VMEM((src_count - 1, blocks * window, NFFT), bf16),
            pltpu.VMEM((blocks * bucket_rows, NFFT), f32),
            pltpu.VMEM((blocks * window, NFFT), f32),
            pltpu.VMEM((OWNERS_STEP * src_count * rows_dest, NFFT), bf16),
            pltpu.VMEM((devices, rows_dest, LAGS), bf16),
            pltpu.VMEM((devices, rows_dest, LAGS), bf16),
            dma((3,)),
            dma((src_count - 1,)),
            dma((src_count - 1,)),
            dma((src_count - 1,)),
            dma((src_count - 1,)),
            dma,
            dma,
        ],
        compiler_params=pltpu.CompilerParams(
            collective_id=0, has_side_effects=True, vmem_limit_bytes=48 * 1024 * 1024
        ),
    )(window_start, segment_row, segments, records, tables, lag_rows)


def solution(mesh):
    in_specs = (P(("rcv", "src"), None), P(("rcv", "src")), P(), P())
    out_specs = P("rcv", "src", None)
    return jax.shard_map(
        functools.partial(on_device, mesh.shape["rcv"], mesh.shape["src"]),
        mesh=mesh,
        in_specs=in_specs,
        out_specs=out_specs,
        check_vma=False,
    )
```

```python
import functools
import math

import jax
import jax.numpy as jnp
import ml_dtypes
import numpy as np
from jax import lax
from jax.experimental import pallas as pl
from jax.experimental.pallas import tpu as pltpu
from jax.sharding import PartitionSpec as P

NFFT = 1024
HALF = NFFT // 2
QUART = NFFT // 4
LAGS = 256
CAP = 2
SEG_PER = 4
LANES = 128
OWNERS_STEP = 4
MESH = pl.DeviceIdType.MESH
ORDER = np.concatenate([np.arange(r, HALF, 4) for r in (0, 2, 1, 3)])


def dft_tables():
    parts = []
    for r, rows in ((0, QUART), (2, QUART), (1, 2 * QUART), (3, 2 * QUART)):
        n = np.arange(rows)
        f = np.arange(r, HALF, 4)
        angles = (n[:, None] * f[None, :] % NFFT) * (2.0 * math.pi / NFFT)
        parts.append(np.concatenate([np.cos(angles), -np.sin(angles)], axis=1))
    table = np.concatenate(parts, axis=0).astype(np.float32)
    high = table.astype(ml_dtypes.bfloat16)
    low = (table - high.astype(np.float32)).astype(ml_dtypes.bfloat16)
    return np.stack([high, low])


def lag_table():
    shifts = np.arange(LAGS) - LAGS // 2
    angles = (ORDER[:, None] * shifts[None, :] % NFFT) * (2.0 * math.pi / NFFT)
    table = np.concatenate([np.cos(angles), -np.sin(angles)], axis=0)
    return table.astype(np.float32).astype(ml_dtypes.bfloat16)


def iota(shape, axis):
    return lax.broadcasted_iota(jnp.int32, shape, axis)


def onehot(mask):
    return jnp.where(mask, 1.0, 0.0).astype(jnp.bfloat16)


def mxu(a, b):
    return jnp.dot(a, b, preferred_element_type=jnp.float32)


def kernel(
    rcv_count,
    src_count,
    tile,
    blocks,
    window_start,
    segment_row_in,
    segments_in,
    records,
    tables,
    lag_rows,
    out,
    segment_row,
    segments,
    x,
    table,
    lags,
    owner_rows,
    starts_out,
    starts_in,
    white,
    sources_out,
    sources_in,
    own,
    sources,
    cross,
    buckets,
    arrived,
    load_sems,
    start_send,
    start_recv,
    source_send,
    source_recv,
    bucket_send,
    bucket_recv,
):
    rcv = lax.axis_index("rcv")
    pos = lax.axis_index("src")
    me = rcv * src_count + pos
    devices = rcv_count * src_count
    window = tile * src_count // 4
    part = window // src_count
    bucket_rows = rcv_count * CAP
    per_row = LANES // tile
    rows_dest = CAP * part

    loads = [
        pltpu.make_async_copy(records, x, load_sems.at[0]),
        pltpu.make_async_copy(tables, table, load_sems.at[1]),
        pltpu.make_async_copy(segments_in, segments, load_sems.at[2]),
        pltpu.make_async_copy(segment_row_in, segment_row, load_sems.at[3]),
        pltpu.make_async_copy(lag_rows, lags, load_sems.at[4]),
    ]
    for load in loads:
        load.start()

    barrier = pltpu.get_barrier_semaphore()

    def greet(step, carry):
        other = lax.rem(me + step, devices)
        pl.semaphore_signal(
            barrier,
            inc=1,
            device_id=(other // src_count, lax.rem(other, src_count)),
            device_id_type=MESH,
        )
        return carry

    lax.fori_loop(1, devices, greet, 0)

    starts_out[...] = jnp.full(starts_out.shape, window_start[0], jnp.int32)

    loads[0].wait()
    pl.semaphore_wait(barrier, devices - 1)

    def start_copy(step):
        other = lax.rem(pos + step, src_count)
        return pltpu.make_async_remote_copy(
            src_ref=starts_out,
            dst_ref=starts_in.at[step - 1],
            send_sem=start_send.at[step - 1],
            recv_sem=start_recv.at[step - 1],
            device_id=(rcv, other),
            device_id_type=MESH,
        )

    for step in range(1, src_count):
        start_copy(step).start()

    quarters = []
    for quarter in range(4):
        quarters.append(
            jnp.concatenate(
                [
                    x[:, block * NFFT + quarter * QUART : block * NFFT + (quarter + 1) * QUART]
                    for block in range(blocks)
                ],
                axis=0,
            )
        )
    even_a, even_b = quarters[0] + quarters[2], quarters[1] + quarters[3]
    odd = jnp.concatenate([quarters[0] - quarters[2], quarters[1] - quarters[3]], axis=1)
    inputs = [even_a + even_b, even_a - even_b, odd, odd]
    loads[1].wait()
    height = blocks * tile
    real_parts, imag_parts = [], []
    first = 0
    for values in inputs:
        depth = values.shape[1]
        high = values.astype(jnp.bfloat16)
        low = (values - high.astype(jnp.float32)).astype(jnp.bfloat16)
        both = mxu(jnp.concatenate([high, low], axis=0), table[0, first : first + depth, :])
        total = both[:height] + both[height:] + mxu(high, table[1, first : first + depth, :])
        first += depth
        real_parts.append(total[:, :LANES])
        imag_parts.append(total[:, LANES:])
    real = jnp.concatenate(real_parts, axis=1)
    imag = jnp.concatenate(imag_parts, axis=1)
    powers = real * real + imag * imag
    mean_power = jnp.mean(powers, axis=1, keepdims=True)
    factor = lax.rsqrt(powers + 0.1 * mean_power + 1e-06)
    white[...] = jnp.concatenate([real * factor, imag * factor], axis=1).astype(jnp.bfloat16)

    def source_copy(step):
        other = lax.rem(pos + step, src_count)
        return pltpu.make_async_remote_copy(
            src_ref=sources_out.at[step - 1],
            dst_ref=sources_in.at[step - 1],
            send_sem=source_send.at[step - 1],
            recv_sem=source_recv.at[step - 1],
            device_id=(rcv, other),
            device_id_type=MESH,
        )

    for step in range(1, src_count):
        other = lax.rem(pos + step, src_count)
        start_copy(src_count - step).wait_recv()
        first_position = starts_in[src_count - step - 1, 0:1, :]
        my_place = pos - jnp.where(pos < other, 0, 1)
        row_id = iota((blocks * window, LANES), 0)
        lane_id = iota((blocks * window, LANES), 1)
        asked = (first_position + row_id % window == my_place * tile + lane_id % tile) & (
            row_id // window == lane_id // tile
        )
        sources_out[step - 1] = mxu(onehot(asked), white[...]).astype(jnp.bfloat16)
        source_copy(step).start()

    loads[2].wait()
    loads[3].wait()
    all_segments = segments[...]

    def look_up(segment, rows):
        return rows + jnp.where(all_segments == segment, segment_row[segment], 0)

    stack_rows = lax.fori_loop(
        0, segment_row.shape[0], look_up, jnp.zeros(all_segments.shape, jnp.int32), unroll=8
    )
    owners = stack_rows // SEG_PER
    slots = stack_rows - owners * SEG_PER
    owner_rows[...] = owners
    lane_a, lane_b = iota((LANES, LANES), 0), iota((LANES, LANES), 1)
    earlier = onehot((lane_a // tile == lane_b // tile) & (lane_a < lane_b))

    mine = owners == rcv
    ranks = mxu(onehot(mine), earlier)
    labels = jnp.zeros((owners.shape[0], LANES), jnp.float32)
    for rank in range(CAP):
        value = jnp.where(mine & (ranks == rank), slots + 1, 0).astype(jnp.bfloat16)
        spread = onehot(
            (lane_a // tile == lane_b // rows_dest % per_row) & (lane_b // part % CAP == rank)
        )
        labels = labels + mxu(value, spread)
    arrivals = devices * rows_dest
    labels = jnp.concatenate([labels] * (arrivals // LANES), axis=1)
    row_id = iota(labels.shape, 0)
    lane_id = iota(labels.shape, 1)
    labels = jnp.sum(
        jnp.where(row_id == lane_id // (rows_dest * per_row), labels, 0.0), axis=0, keepdims=True
    )
    out_id = iota((SEG_PER * part, arrivals), 0)
    lane_id = iota((SEG_PER * part, arrivals), 1)
    chosen = (labels == (out_id // part + 1).astype(jnp.float32)) & (
        out_id % part == lane_id % part
    )
    summing = jnp.where(chosen, 1.0, 0.0)
    counts = jnp.sum(summing, axis=1, keepdims=True)
    out_scale = 1.0 / jnp.sqrt(jnp.maximum(counts, 1.0))
    summing = summing.astype(jnp.bfloat16)

    tile_owners = owner_rows[pl.ds(me // per_row, 1), :]
    bucket_id = iota((bucket_rows, LANES), 0)
    held = bucket_id // CAP == tile_owners
    tile_ranks = mxu(onehot(held), earlier)
    placed = onehot(held & (tile_ranks == (bucket_id % CAP).astype(jnp.float32)))
    fold = onehot(
        (lane_a // tile == lax.rem(me, per_row)) & (lane_a % tile == lane_b % tile)
    )
    placed = mxu(placed, fold)
    placed = jnp.concatenate([placed] * blocks, axis=0)
    placed = jnp.where(
        iota(placed.shape, 0) // bucket_rows == iota(placed.shape, 1) // tile, placed, 0.0
    ).astype(jnp.bfloat16)

    own[...] = mxu(placed, white[...])

    loads[4].wait()
    for step in range(1, src_count):
        source_copy(step).wait_recv()
    total = sources_in[0].astype(jnp.float32)
    for step in range(2, src_count):
        total = total + sources_in[step - 1].astype(jnp.float32)
    sources[...] = total

    scale = 1.0 / math.sqrt(blocks * HALF)
    steps = rcv_count // OWNERS_STEP
    group_rows = src_count * rows_dest

    def bucket_copy(owner, place):
        return pltpu.make_async_remote_copy(
            src_ref=buckets.at[owner * src_count + place],
            dst_ref=arrived.at[me],
            send_sem=bucket_send,
            recv_sem=bucket_recv,
            device_id=(owner, place),
            device_id_type=MESH,
        )

    def owner_step(step, carry):
        chunk = lax.rem(rcv // OWNERS_STEP + 1 + step, steps)

        def cross_step(index, inner):
            re_cols = pl.ds(pl.multiple_of(index * LANES, LANES), LANES)
            im_cols = pl.ds(pl.multiple_of(HALF + index * LANES, LANES), LANES)
            group = OWNERS_STEP * CAP
            left = []
            for block in range(blocks):
                first_row = pl.multiple_of(block * bucket_rows + chunk * group, group)
                rows = pl.ds(first_row, group)
                left.append((own[rows, re_cols], own[rows, im_cols]))
            for place in range(src_count):
                right = []
                for block in range(blocks):
                    rows = slice(block * window + place * part, block * window + (place + 1) * part)
                    right.append((sources[rows, re_cols], sources[rows, im_cols]))
                for owner in range(OWNERS_STEP):
                    reals, imags = [], []
                    for rank in range(CAP):
                        row = slice(owner * CAP + rank, owner * CAP + rank + 1)
                        re_sum, im_sum = None, None
                        for block in range(blocks):
                            left_re, left_im = left[block][0][row], left[block][1][row]
                            right_re, right_im = right[block]
                            re_term = left_re * right_re + left_im * right_im
                            im_term = left_re * right_im - left_im * right_re
                            re_sum = re_term if re_sum is None else re_sum + re_term
                            im_sum = im_term if im_sum is None else im_sum + im_term
                        reals.append(re_sum)
                        imags.append(im_sum)
                    at = owner * group_rows + place * rows_dest
                    rows = slice(at, at + rows_dest)
                    cross[rows, re_cols] = jnp.concatenate(reals, axis=0).astype(jnp.bfloat16)
                    cross[rows, im_cols] = jnp.concatenate(imags, axis=0).astype(jnp.bfloat16)
            return inner

        lax.fori_loop(0, HALF // LANES, cross_step, 0)
        rows = (mxu(cross[...], lags[...]) * scale).astype(jnp.bfloat16)
        dests = OWNERS_STEP * src_count
        buckets[pl.ds(chunk * dests, dests)] = rows.reshape(dests, rows_dest, LAGS)

        def send(index, inner):
            dest = chunk * dests + index

            @pl.when(dest != me)
            def _():
                bucket_copy(dest // src_count, lax.rem(dest, src_count)).start()

            return inner

        lax.fori_loop(0, dests, send, 0)
        return carry

    lax.fori_loop(0, steps, owner_step, 0)
    arrived[pl.ds(me, 1)] = buckets[pl.ds(me, 1)]

    others = pl.ds(0, devices - 1)
    pltpu.make_async_copy(arrived.at[others], arrived.at[others], bucket_recv).wait()
    stacked = mxu(summing, arrived[...].reshape(arrivals, LAGS)) * out_scale
    out[...] = stacked.reshape(SEG_PER, part, LAGS)

    pltpu.make_async_copy(buckets.at[others], buckets.at[others], bucket_send).wait()
    for step in range(1, src_count):
        start_copy(step).wait_send()
        source_copy(step).wait_send()


def on_device(rcv_count, src_count, records, window_start, channel_segment, segment_row):
    tile, samples = records.shape
    blocks = samples // NFFT
    devices = rcv_count * src_count
    window = tile * src_count // 4
    part = window // src_count
    rows_dest = CAP * part
    bucket_rows = rcv_count * CAP
    segments = channel_segment.reshape(-1, LANES)
    tables = jnp.asarray(dft_tables())
    lag_rows = jnp.asarray(lag_table())
    smem = pl.BlockSpec(memory_space=pltpu.SMEM)
    vmem = pl.BlockSpec(memory_space=pltpu.VMEM)
    hbm = pl.BlockSpec(memory_space=pltpu.HBM)
    bf16, f32, i32 = jnp.bfloat16, jnp.float32, jnp.int32
    dma = pltpu.SemaphoreType.DMA
    return pl.pallas_call(
        functools.partial(kernel, rcv_count, src_count, tile, blocks),
        out_shape=jax.ShapeDtypeStruct((SEG_PER, part, LAGS), f32),
        in_specs=[smem, hbm, hbm, hbm, hbm, hbm],
        out_specs=vmem,
        scratch_shapes=[
            pltpu.SMEM(segment_row.shape, i32),
            pltpu.VMEM(segments.shape, i32),
            pltpu.VMEM(records.shape, f32),
            pltpu.VMEM(tables.shape, bf16),
            pltpu.VMEM(lag_rows.shape, bf16),
            pltpu.VMEM(segments.shape, i32),
            pltpu.VMEM((8, LANES), i32),
            pltpu.VMEM((src_count - 1, 8, LANES), i32),
            pltpu.VMEM((blocks * tile, NFFT), bf16),
            pltpu.VMEM((src_count - 1, blocks * window, NFFT), bf16),
            pltpu.VMEM((src_count - 1, blocks * window, NFFT), bf16),
            pltpu.VMEM((blocks * bucket_rows, NFFT), f32),
            pltpu.VMEM((blocks * window, NFFT), f32),
            pltpu.VMEM((OWNERS_STEP * src_count * rows_dest, NFFT), bf16),
            pltpu.VMEM((devices, rows_dest, LAGS), bf16),
            pltpu.VMEM((devices, rows_dest, LAGS), bf16),
            dma((5,)),
            dma((src_count - 1,)),
            dma((src_count - 1,)),
            dma((src_count - 1,)),
            dma((src_count - 1,)),
            dma,
            dma,
        ],
        compiler_params=pltpu.CompilerParams(
            collective_id=0, has_side_effects=True, vmem_limit_bytes=62 * 1024 * 1024
        ),
    )(window_start, segment_row, segments, records, tables, lag_rows)


def solution(mesh):
    in_specs = (P(("rcv", "src"), None), P(("rcv", "src")), P(), P())
    out_specs = P("rcv", "src", None)
    return jax.shard_map(
        functools.partial(on_device, mesh.shape["rcv"], mesh.shape["src"]),
        mesh=mesh,
        in_specs=in_specs,
        out_specs=out_specs,
        check_vma=False,
    )
```

```python
import functools
import math

import jax
import jax.numpy as jnp
import ml_dtypes
import numpy as np
from jax import lax
from jax.experimental import pallas as pl
from jax.experimental.pallas import tpu as pltpu
from jax.sharding import PartitionSpec as P

NFFT = 1024
HALF = NFFT // 2
QUART = NFFT // 4
LAGS = 256
CAP = 2
SEG_PER = 4
LANES = 128
OWNERS_STEP = 4
DELAY = 2
MESH = pl.DeviceIdType.MESH
ORDER = np.concatenate([np.arange(r, HALF, 4) for r in (0, 2, 1, 3)])


def dft_tables():
    parts = []
    for r, rows in ((0, QUART), (2, QUART), (1, 2 * QUART), (3, 2 * QUART)):
        n = np.arange(rows)
        f = np.arange(r, HALF, 4)
        angles = (n[:, None] * f[None, :] % NFFT) * (2.0 * math.pi / NFFT)
        parts.append(np.concatenate([np.cos(angles), -np.sin(angles)], axis=1))
    table = np.concatenate(parts, axis=0).astype(np.float32)
    high = table.astype(ml_dtypes.bfloat16)
    low = (table - high.astype(np.float32)).astype(ml_dtypes.bfloat16)
    return np.stack([high, low])


def lag_table():
    shifts = np.arange(LAGS) - LAGS // 2
    angles = (ORDER[:, None] * shifts[None, :] % NFFT) * (2.0 * math.pi / NFFT)
    table = np.concatenate([np.cos(angles), -np.sin(angles)], axis=0)
    return table.astype(np.float32).astype(ml_dtypes.bfloat16)


def iota(shape, axis):
    return lax.broadcasted_iota(jnp.int32, shape, axis)


def div(a, b):
    return lax.shift_right_logical(a, b.bit_length() - 1) if b & (b - 1) == 0 else a // b


def mod(a, b):
    return a & (b - 1) if b & (b - 1) == 0 else a % b


def onehot(mask):
    return jnp.where(mask, 1.0, 0.0).astype(jnp.bfloat16)


def mxu(a, b):
    return jnp.dot(a, b, preferred_element_type=jnp.float32)


def kernel(
    rcv_count,
    src_count,
    tile,
    blocks,
    window_start,
    segment_row_in,
    segments_in,
    records,
    tables,
    lag_rows,
    out,
    segment_row,
    segments,
    x,
    table,
    lags,
    owner_rows,
    summing,
    starts_out,
    starts_in,
    white,
    sources_out,
    sources_in,
    own,
    sources,
    cross,
    buckets,
    arrived,
    partial,
    arrived_sums,
    load_sems,
    start_send,
    start_recv,
    source_send,
    source_recv,
    bucket_send,
    bucket_recv,
    sum_send,
    sum_recv,
):
    rcv = lax.axis_index("rcv")
    pos = lax.axis_index("src")
    me = rcv * src_count + pos
    window = tile * src_count // 4
    part = window // src_count
    bucket_rows = rcv_count * CAP
    per_row = LANES // tile
    rows_dest = CAP * part

    loads = [
        pltpu.make_async_copy(records, x, load_sems.at[0]),
        pltpu.make_async_copy(tables, table, load_sems.at[1]),
        pltpu.make_async_copy(segments_in, segments, load_sems.at[2]),
        pltpu.make_async_copy(segment_row_in, segment_row, load_sems.at[3]),
        pltpu.make_async_copy(lag_rows, lags, load_sems.at[4]),
    ]
    for load in loads:
        load.start()

    barrier = pltpu.get_barrier_semaphore()

    steps = rcv_count // OWNERS_STEP
    plane_size = OWNERS_STEP * src_count
    plane = div(rcv, OWNERS_STEP)
    spot = lax.rem(me, plane_size)

    def signal(plane_id, spot_id):
        pl.semaphore_signal(
            barrier,
            inc=1,
            device_id=(
                plane_id * OWNERS_STEP + spot_id // src_count,
                lax.rem(spot_id, src_count),
            ),
            device_id_type=MESH,
        )

    def greet_plane(step, carry):
        signal(plane, lax.rem(spot + step, plane_size))
        return carry

    def greet_planes(step, carry):
        signal(lax.rem(plane + step, steps), spot)
        return carry

    lax.fori_loop(1, plane_size, greet_plane, 0)
    lax.fori_loop(1, steps, greet_planes, 0)

    starts_out[...] = jnp.full(starts_out.shape, window_start[0], jnp.int32)

    loads[0].wait()
    pl.semaphore_wait(barrier, plane_size + steps - 2)

    def start_copy(step):
        other = lax.rem(pos + step, src_count)
        return pltpu.make_async_remote_copy(
            src_ref=starts_out,
            dst_ref=starts_in.at[step - 1],
            send_sem=start_send.at[step - 1],
            recv_sem=start_recv.at[step - 1],
            device_id=(rcv, other),
            device_id_type=MESH,
        )

    for step in range(1, src_count):
        start_copy(step).start()

    quarters = []
    for quarter in range(4):
        quarters.append(
            jnp.concatenate(
                [
                    x[:, block * NFFT + quarter * QUART : block * NFFT + (quarter + 1) * QUART]
                    for block in range(blocks)
                ],
                axis=0,
            )
        )
    even_a, even_b = quarters[0] + quarters[2], quarters[1] + quarters[3]
    odd = jnp.concatenate([quarters[0] - quarters[2], quarters[1] - quarters[3]], axis=1)
    inputs = [even_a + even_b, even_a - even_b, odd, odd]
    loads[1].wait()
    height = blocks * tile
    real_parts, imag_parts = [], []
    first = 0
    for values in inputs:
        depth = values.shape[1]
        high = values.astype(jnp.bfloat16)
        low = (values - high.astype(jnp.float32)).astype(jnp.bfloat16)
        both = mxu(jnp.concatenate([high, low], axis=0), table[0, first : first + depth, :])
        total = both[:height] + both[height:] + mxu(high, table[1, first : first + depth, :])
        first += depth
        real_parts.append(total[:, :LANES])
        imag_parts.append(total[:, LANES:])
    real = jnp.concatenate(real_parts, axis=1)
    imag = jnp.concatenate(imag_parts, axis=1)
    powers = real * real + imag * imag
    mean_power = jnp.mean(powers, axis=1, keepdims=True)
    factor = lax.rsqrt(powers + 0.1 * mean_power + 1e-06)
    white[...] = jnp.concatenate([real * factor, imag * factor], axis=1).astype(jnp.bfloat16)

    def source_copy(step):
        other = lax.rem(pos + step, src_count)
        return pltpu.make_async_remote_copy(
            src_ref=sources_out.at[step - 1],
            dst_ref=sources_in.at[step - 1],
            send_sem=source_send.at[step - 1],
            recv_sem=source_recv.at[step - 1],
            device_id=(rcv, other),
            device_id_type=MESH,
        )

    for step in range(1, src_count):
        other = lax.rem(pos + step, src_count)
        start_copy(src_count - step).wait_recv()
        first_position = starts_in[src_count - step - 1, 0:1, :]
        my_place = pos - jnp.where(pos < other, 0, 1)
        row_id = iota((blocks * window, LANES), 0)
        lane_id = iota((blocks * window, LANES), 1)
        asked = (first_position + mod(row_id, window) == my_place * tile + mod(lane_id, tile)) & (
            div(row_id, window) == div(lane_id, tile)
        )
        sources_out[step - 1] = mxu(onehot(asked), white[...]).astype(jnp.bfloat16)
        source_copy(step).start()

    loads[2].wait()
    loads[3].wait()
    all_segments = segments[...]

    def look_up(segment, rows):
        return rows + jnp.where(all_segments == segment, segment_row[segment], 0)

    stack_rows = lax.fori_loop(
        0, segment_row.shape[0], look_up, jnp.zeros(all_segments.shape, jnp.int32), unroll=8
    )
    owners = div(stack_rows, SEG_PER)
    slots = mod(stack_rows, SEG_PER)
    owner_rows[...] = owners
    lane_a, lane_b = iota((LANES, LANES), 0), iota((LANES, LANES), 1)
    earlier = onehot((div(lane_a, tile) == div(lane_b, tile)) & (lane_a < lane_b))

    out_rows = SEG_PER * part
    out_id = iota((out_rows, 1), 0)
    counts = jnp.zeros((out_rows, 1), jnp.float32)
    for slot in range(SEG_PER):
        members = jnp.where(stack_rows == rcv * SEG_PER + slot, 1.0, 0.0)
        members = jnp.sum(jnp.sum(members, axis=0, keepdims=True), axis=1, keepdims=True)
        counts = counts + jnp.where(div(out_id, part) == slot, members, 0.0)
    out_scale = 1.0 / jnp.sqrt(jnp.maximum(counts, 1.0))

    plane_lanes = plane_size * rows_dest
    row_count = owners.shape[0]
    owner_here = lax.rem(rcv, OWNERS_STEP)
    mine = jnp.concatenate(
        [owners == step * OWNERS_STEP + owner_here for step in range(steps)], axis=0
    )
    all_slots = jnp.concatenate([slots] * steps, axis=0)
    ranks = mxu(onehot(mine), earlier)
    labels = jnp.zeros(mine.shape, jnp.float32)
    for rank in range(CAP):
        value = jnp.where(mine & (ranks == rank), all_slots + 1, 0).astype(jnp.bfloat16)
        spread = onehot(
            (div(lane_a, tile) == mod(div(lane_b, rows_dest), per_row))
            & (mod(div(lane_b, part), CAP) == rank)
        )
        labels = labels + mxu(value, spread)
    labels = jnp.concatenate([labels] * (plane_lanes // LANES), axis=1)
    wanted = plane * (plane_size // per_row) + div(
        iota((row_count, plane_lanes), 1), rows_dest * per_row
    )
    wanted = iota((row_count, plane_lanes), 0) == wanted
    out_id = iota((out_rows, plane_lanes), 0)
    lane_id = iota((out_rows, plane_lanes), 1)
    aligned = mod(out_id, part) == mod(lane_id, part)
    slot_id = (div(out_id, part) + 1).astype(jnp.float32)
    for step in range(steps):
        rows = labels[step * row_count : (step + 1) * row_count]
        label = jnp.sum(jnp.where(wanted, rows, 0.0), axis=0, keepdims=True)
        summing[step] = onehot((label == slot_id) & aligned)

    tile_owners = owner_rows[pl.ds(div(me, per_row), 1), :]
    bucket_id = iota((bucket_rows, LANES), 0)
    held = div(bucket_id, CAP) == tile_owners
    tile_ranks = mxu(onehot(held), earlier)
    placed = onehot(held & (tile_ranks == mod(bucket_id, CAP).astype(jnp.float32)))
    fold = onehot(
        (div(lane_a, tile) == lax.rem(me, per_row)) & (mod(lane_a, tile) == mod(lane_b, tile))
    )
    placed = mxu(placed, fold)
    lane_block = div(iota((bucket_rows, LANES), 1), tile)
    placed = jnp.concatenate(
        [jnp.where(lane_block == block, placed, 0.0) for block in range(blocks)], axis=0
    ).astype(jnp.bfloat16)

    own[...] = mxu(placed, white[...])

    loads[4].wait()
    for step in range(1, src_count):
        source_copy(step).wait_recv()
    total = sources_in[0].astype(jnp.float32)
    for step in range(2, src_count):
        total = total + sources_in[step - 1].astype(jnp.float32)
    sources[...] = total

    scale = 1.0 / math.sqrt(blocks * HALF)
    group_rows = src_count * rows_dest

    def bucket_copy(chunk, other):
        return pltpu.make_async_remote_copy(
            src_ref=buckets.at[chunk * plane_size + other],
            dst_ref=arrived.at[chunk, spot],
            send_sem=bucket_send,
            recv_sem=bucket_recv.at[chunk],
            device_id=(plane * OWNERS_STEP + other // src_count, lax.rem(other, src_count)),
            device_id_type=MESH,
        )

    def sum_copy(chunk):
        return pltpu.make_async_remote_copy(
            src_ref=partial.at[chunk],
            dst_ref=arrived_sums.at[plane],
            send_sem=sum_send,
            recv_sem=sum_recv,
            device_id=(chunk * OWNERS_STEP + owner_here, pos),
            device_id_type=MESH,
        )

    def chunk_of(step):
        return lax.rem(plane + 1 + step, steps)

    def plane_sum(chunk):
        arrived[chunk, pl.ds(spot, 1)] = buckets[pl.ds(chunk * plane_size + spot, 1)]
        landed = arrived.at[chunk, pl.ds(0, plane_size - 1)]
        pltpu.make_async_copy(landed, landed, bucket_recv.at[chunk]).wait()
        return mxu(summing[chunk], arrived[chunk].reshape(plane_lanes, LAGS))

    def pass_on(step):
        chunk = chunk_of(step)
        partial[chunk] = plane_sum(chunk).astype(jnp.bfloat16)
        sum_copy(chunk).start()

    def owner_step(step, carry):
        chunk = chunk_of(step)

        def cross_step(index, inner):
            re_cols = pl.ds(pl.multiple_of(index * LANES, LANES), LANES)
            im_cols = pl.ds(pl.multiple_of(HALF + index * LANES, LANES), LANES)
            group = OWNERS_STEP * CAP
            left = []
            for block in range(blocks):
                first_row = pl.multiple_of(block * bucket_rows + chunk * group, group)
                rows = pl.ds(first_row, group)
                left.append((own[rows, re_cols], own[rows, im_cols]))
            for place in range(src_count):
                right = []
                for block in range(blocks):
                    rows = slice(block * window + place * part, block * window + (place + 1) * part)
                    right.append((sources[rows, re_cols], sources[rows, im_cols]))
                for owner in range(OWNERS_STEP):
                    reals, imags = [], []
                    for rank in range(CAP):
                        row = slice(owner * CAP + rank, owner * CAP + rank + 1)
                        re_sum, im_sum = None, None
                        for block in range(blocks):
                            left_re, left_im = left[block][0][row], left[block][1][row]
                            right_re, right_im = right[block]
                            re_term = left_re * right_re + left_im * right_im
                            im_term = left_re * right_im - left_im * right_re
                            re_sum = re_term if re_sum is None else re_sum + re_term
                            im_sum = im_term if im_sum is None else im_sum + im_term
                        reals.append(re_sum)
                        imags.append(im_sum)
                    at = owner * group_rows + place * rows_dest
                    rows = slice(at, at + rows_dest)
                    cross[rows, re_cols] = jnp.concatenate(reals, axis=0).astype(jnp.bfloat16)
                    cross[rows, im_cols] = jnp.concatenate(imags, axis=0).astype(jnp.bfloat16)
            return inner

        lax.fori_loop(0, HALF // LANES, cross_step, 0)
        rows = (mxu(cross[...], lags[...]) * scale).astype(jnp.bfloat16)
        buckets[pl.ds(chunk * plane_size, plane_size)] = rows.reshape(plane_size, rows_dest, LAGS)

        def send(index, inner):
            bucket_copy(chunk, lax.rem(spot + index, plane_size)).start()
            return inner

        lax.fori_loop(1, plane_size, send, 0)

        @pl.when(step >= DELAY)
        def _():
            pass_on(step - DELAY)

        return carry

    lax.fori_loop(0, steps, owner_step, 0)
    for step in range(steps - DELAY, steps - 1):
        pass_on(step)
    stacked = plane_sum(plane)

    others = pl.ds(0, steps - 1)
    landed = arrived_sums.at[others]
    pltpu.make_async_copy(landed, landed, sum_recv).wait()
    arrived_sums[plane] = jnp.zeros((out_rows, LAGS), jnp.bfloat16)
    for step in range(steps):
        stacked = stacked + arrived_sums[step].astype(jnp.float32)
    out[...] = (stacked * out_scale).reshape(SEG_PER, part, LAGS)

    sent = partial.at[others]
    pltpu.make_async_copy(sent, sent, sum_send).wait()
    sent = buckets.at[pl.ds(0, steps * (plane_size - 1))]
    pltpu.make_async_copy(sent, sent, bucket_send).wait()
    for step in range(1, src_count):
        start_copy(step).wait_send()
        source_copy(step).wait_send()


def on_device(rcv_count, src_count, records, window_start, channel_segment, segment_row):
    tile, samples = records.shape
    blocks = samples // NFFT
    devices = rcv_count * src_count
    window = tile * src_count // 4
    part = window // src_count
    rows_dest = CAP * part
    bucket_rows = rcv_count * CAP
    steps = rcv_count // OWNERS_STEP
    plane_size = OWNERS_STEP * src_count
    segments = channel_segment.reshape(-1, LANES)
    tables = jnp.asarray(dft_tables())
    lag_rows = jnp.asarray(lag_table())
    smem = pl.BlockSpec(memory_space=pltpu.SMEM)
    vmem = pl.BlockSpec(memory_space=pltpu.VMEM)
    hbm = pl.BlockSpec(memory_space=pltpu.HBM)
    bf16, f32, i32 = jnp.bfloat16, jnp.float32, jnp.int32
    dma = pltpu.SemaphoreType.DMA
    return pl.pallas_call(
        functools.partial(kernel, rcv_count, src_count, tile, blocks),
        out_shape=jax.ShapeDtypeStruct((SEG_PER, part, LAGS), f32),
        in_specs=[smem, hbm, hbm, hbm, hbm, hbm],
        out_specs=vmem,
        scratch_shapes=[
            pltpu.SMEM(segment_row.shape, i32),
            pltpu.VMEM(segments.shape, i32),
            pltpu.VMEM(records.shape, f32),
            pltpu.VMEM(tables.shape, bf16),
            pltpu.VMEM(lag_rows.shape, bf16),
            pltpu.VMEM(segments.shape, i32),
            pltpu.VMEM((steps, SEG_PER * part, plane_size * rows_dest), bf16),
            pltpu.VMEM((8, LANES), i32),
            pltpu.VMEM((src_count - 1, 8, LANES), i32),
            pltpu.VMEM((blocks * tile, NFFT), bf16),
            pltpu.VMEM((src_count - 1, blocks * window, NFFT), bf16),
            pltpu.VMEM((src_count - 1, blocks * window, NFFT), bf16),
            pltpu.VMEM((blocks * bucket_rows, NFFT), f32),
            pltpu.VMEM((blocks * window, NFFT), f32),
            pltpu.VMEM((OWNERS_STEP * src_count * rows_dest, NFFT), bf16),
            pltpu.VMEM((devices, rows_dest, LAGS), bf16),
            pltpu.VMEM((steps, plane_size, rows_dest, LAGS), bf16),
            pltpu.VMEM((steps, SEG_PER * part, LAGS), bf16),
            pltpu.VMEM((steps, SEG_PER * part, LAGS), bf16),
            dma((5,)),
            dma((src_count - 1,)),
            dma((src_count - 1,)),
            dma((src_count - 1,)),
            dma((src_count - 1,)),
            dma,
            dma((steps,)),
            dma,
            dma,
        ],
        compiler_params=pltpu.CompilerParams(
            collective_id=0, has_side_effects=True, vmem_limit_bytes=62 * 1024 * 1024
        ),
    )(window_start, segment_row, segments, records, tables, lag_rows)


def solution(mesh):
    in_specs = (P(("rcv", "src"), None), P(("rcv", "src")), P(), P())
    out_specs = P("rcv", "src", None)
    return jax.shard_map(
        functools.partial(on_device, mesh.shape["rcv"], mesh.shape["src"]),
        mesh=mesh,
        in_specs=in_specs,
        out_specs=out_specs,
        check_vma=False,
    )
```

```python
import functools
import math

import jax
import jax.numpy as jnp
import ml_dtypes
import numpy as np
from jax import lax
from jax.experimental import pallas as pl
from jax.experimental.pallas import tpu as pltpu
from jax.sharding import PartitionSpec as P

NFFT = 1024
HALF = NFFT // 2
QUART = NFFT // 4
LAGS = 256
CAP = 2
SEG_PER = 4
LANES = 128
OWNERS_STEP = 4
OWNERS_SEND = 8
MESH = pl.DeviceIdType.MESH
ORDER = np.concatenate([np.arange(r, HALF, 4) for r in (0, 2, 1, 3)])


def dft_tables():
    parts = []
    for r, rows in ((0, QUART), (2, QUART), (1, 2 * QUART), (3, 2 * QUART)):
        n = np.arange(rows)
        f = np.arange(r, HALF, 4)
        angles = (n[:, None] * f[None, :] % NFFT) * (2.0 * math.pi / NFFT)
        parts.append(np.concatenate([np.cos(angles), -np.sin(angles)], axis=1))
    table = np.concatenate(parts, axis=0).astype(np.float32)
    high = table.astype(ml_dtypes.bfloat16)
    low = (table - high.astype(np.float32)).astype(ml_dtypes.bfloat16)
    return np.stack([high, low])


def lag_table():
    shifts = np.arange(LAGS) - LAGS // 2
    angles = (ORDER[:, None] * shifts[None, :] % NFFT) * (2.0 * math.pi / NFFT)
    table = np.concatenate([np.cos(angles), -np.sin(angles)], axis=0)
    return table.astype(np.float32).astype(ml_dtypes.bfloat16)


def iota(shape, axis):
    return lax.broadcasted_iota(jnp.int32, shape, axis)


def div(a, b):
    return lax.shift_right_logical(a, b.bit_length() - 1) if b & (b - 1) == 0 else a // b


def mod(a, b):
    return a & (b - 1) if b & (b - 1) == 0 else a % b


def onehot(mask):
    return jnp.where(mask, 1.0, 0.0).astype(jnp.bfloat16)


def mxu(a, b):
    return jnp.dot(a, b, preferred_element_type=jnp.float32)


def kernel(
    rcv_count,
    src_count,
    tile,
    blocks,
    window_start,
    segment_row_in,
    segments_in,
    records,
    tables,
    lag_rows,
    out,
    segment_row,
    segments,
    x,
    table,
    lags,
    owner_rows,
    summing,
    out_scale,
    starts_out,
    starts_in,
    white,
    sources_out,
    sources_in,
    own,
    sources,
    cross,
    buckets,
    arrived,
    load_sems,
    start_send,
    start_recv,
    source_send,
    source_recv,
    bucket_send,
    bucket_recv,
):
    rcv = lax.axis_index("rcv")
    pos = lax.axis_index("src")
    me = rcv * src_count + pos
    devices = rcv_count * src_count
    window = tile * src_count // 4
    part = window // src_count
    bucket_rows = rcv_count * CAP
    per_row = LANES // tile
    rows_dest = CAP * part

    loads = [
        pltpu.make_async_copy(records, x, load_sems.at[0]),
        pltpu.make_async_copy(tables, table, load_sems.at[1]),
        pltpu.make_async_copy(segments_in, segments, load_sems.at[2]),
        pltpu.make_async_copy(segment_row_in, segment_row, load_sems.at[3]),
        pltpu.make_async_copy(lag_rows, lags, load_sems.at[4]),
    ]
    for load in loads:
        load.start()

    barrier = pltpu.get_barrier_semaphore()

    def greet(step, carry):
        other = mod(me + step, devices)
        pl.semaphore_signal(
            barrier,
            inc=1,
            device_id=(div(other, src_count), mod(other, src_count)),
            device_id_type=MESH,
        )
        return carry

    lax.fori_loop(1, devices, greet, 0)

    starts_out[...] = jnp.full(starts_out.shape, window_start[0], jnp.int32)

    loads[0].wait()
    pl.semaphore_wait(barrier, devices - 1)

    def start_copy(step):
        other = lax.rem(pos + step, src_count)
        return pltpu.make_async_remote_copy(
            src_ref=starts_out,
            dst_ref=starts_in.at[step - 1],
            send_sem=start_send.at[step - 1],
            recv_sem=start_recv.at[step - 1],
            device_id=(rcv, other),
            device_id_type=MESH,
        )

    for step in range(1, src_count):
        start_copy(step).start()

    quarters = []
    for quarter in range(4):
        quarters.append(
            jnp.concatenate(
                [
                    x[:, block * NFFT + quarter * QUART : block * NFFT + (quarter + 1) * QUART]
                    for block in range(blocks)
                ],
                axis=0,
            )
        )
    even_a, even_b = quarters[0] + quarters[2], quarters[1] + quarters[3]
    odd = jnp.concatenate([quarters[0] - quarters[2], quarters[1] - quarters[3]], axis=1)
    inputs = [even_a + even_b, even_a - even_b, odd, odd]
    loads[1].wait()
    height = blocks * tile
    real_parts, imag_parts = [], []
    first = 0
    for values in inputs:
        depth = values.shape[1]
        high = values.astype(jnp.bfloat16)
        low = (values - high.astype(jnp.float32)).astype(jnp.bfloat16)
        both = mxu(jnp.concatenate([high, low], axis=0), table[0, first : first + depth, :])
        total = both[:height] + both[height:] + mxu(high, table[1, first : first + depth, :])
        first += depth
        real_parts.append(total[:, :LANES])
        imag_parts.append(total[:, LANES:])
    real = jnp.concatenate(real_parts, axis=1)
    imag = jnp.concatenate(imag_parts, axis=1)
    powers = real * real + imag * imag
    mean_power = jnp.mean(powers, axis=1, keepdims=True)
    factor = lax.rsqrt(powers + 0.1 * mean_power + 1e-06)
    white[...] = jnp.concatenate([real * factor, imag * factor], axis=1).astype(jnp.bfloat16)

    def source_copy(step, column):
        other = lax.rem(pos + step, src_count)
        return pltpu.make_async_remote_copy(
            src_ref=sources_out.at[step - 1, column],
            dst_ref=sources_in.at[step - 1, column],
            send_sem=source_send.at[step - 1, column],
            recv_sem=source_recv.at[step - 1, column],
            device_id=(rcv, other),
            device_id_type=MESH,
        )

    columns = HALF // LANES
    row_id = iota((blocks * window, LANES), 0)
    lane_id = iota((blocks * window, LANES), 1)
    same_block = div(row_id, window) == div(lane_id, tile)
    offset = mod(row_id, window) - mod(lane_id, tile)
    for step in range(1, src_count):
        other = lax.rem(pos + step, src_count)
        start_copy(src_count - step).wait_recv()
        first_position = starts_in[src_count - step - 1, 0:1, :]
        my_place = pos - jnp.where(pos < other, 0, 1)
        asked = onehot(same_block & (offset == my_place * tile - first_position))
        for column in range(columns):
            for half in range(2):
                lanes = slice(half * HALF + column * LANES, half * HALF + (column + 1) * LANES)
                sources_out[step - 1, column, :, half * LANES : (half + 1) * LANES] = mxu(
                    asked, white[:, lanes]
                ).astype(jnp.bfloat16)
            source_copy(step, column).start()

    loads[2].wait()
    loads[3].wait()
    all_segments = segments[...]

    def look_up(segment, rows):
        return rows + jnp.where(all_segments == segment, segment_row[segment], 0)

    stack_rows = lax.fori_loop(
        0, segment_row.shape[0], look_up, jnp.zeros(all_segments.shape, jnp.int32), unroll=8
    )
    owners = div(stack_rows, SEG_PER)
    slots = mod(stack_rows, SEG_PER)
    owner_rows[...] = owners
    lane_a, lane_b = iota((LANES, LANES), 0), iota((LANES, LANES), 1)
    earlier = onehot((div(lane_a, tile) == div(lane_b, tile)) & (lane_a < lane_b))

    tile_owners = owner_rows[pl.ds(div(me, per_row), 1), :]
    bucket_id = iota((bucket_rows, LANES), 0)
    held = div(bucket_id, CAP) == tile_owners
    tile_ranks = mxu(onehot(held), earlier)
    placed = onehot(held & (tile_ranks == mod(bucket_id, CAP).astype(jnp.float32)))
    fold = onehot(
        (div(lane_a, tile) == lax.rem(me, per_row)) & (mod(lane_a, tile) == mod(lane_b, tile))
    )
    placed = mxu(placed, fold)
    lane_block = div(iota((bucket_rows, LANES), 1), tile)
    placed = jnp.concatenate(
        [jnp.where(lane_block == block, placed, 0.0) for block in range(blocks)], axis=0
    ).astype(jnp.bfloat16)

    mine = owners == rcv
    ranks = mxu(onehot(mine), earlier)
    labels = jnp.zeros((owners.shape[0], LANES), jnp.float32)
    for rank in range(CAP):
        value = jnp.where(mine & (ranks == rank), slots + 1, 0).astype(jnp.bfloat16)
        spread = onehot(
            (div(lane_a, tile) == mod(div(lane_b, rows_dest), per_row))
            & (mod(div(lane_b, part), CAP) == rank)
        )
        labels = labels + mxu(value, spread)
    arrivals = devices * rows_dest
    labels = jnp.concatenate([labels] * (arrivals // LANES), axis=1)
    wanted = iota(labels.shape, 0) == div(iota(labels.shape, 1), rows_dest * per_row)
    labels = jnp.sum(jnp.where(wanted, labels, 0.0), axis=0, keepdims=True)
    out_rows = SEG_PER * part
    out_id = iota((out_rows, arrivals), 0)
    lane_id = iota((out_rows, arrivals), 1)
    chosen = (labels == (div(out_id, part) + 1).astype(jnp.float32)) & (
        mod(out_id, part) == mod(lane_id, part)
    )
    chosen = jnp.where(chosen, 1.0, 0.0)
    counts = jnp.sum(chosen, axis=1, keepdims=True)
    out_scale[...] = jnp.broadcast_to(
        1.0 / jnp.sqrt(jnp.maximum(counts, 1.0)), (out_rows, LAGS)
    )
    summing[...] = chosen.astype(jnp.bfloat16)

    own[...] = mxu(placed, white[...])

    group = OWNERS_STEP * CAP
    group_rows = src_count * rows_dest
    for column in range(columns):
        re_cols = slice(column * LANES, (column + 1) * LANES)
        im_cols = slice(HALF + column * LANES, HALF + (column + 1) * LANES)
        for step in range(1, src_count):
            source_copy(step, column).wait_recv()
        total = sources_in[0, column].astype(jnp.float32)
        for step in range(2, src_count):
            total = total + sources_in[step - 1, column].astype(jnp.float32)
        sources[...] = total

        def cross_step(chunk, carry):
            left = []
            for block in range(blocks):
                first_row = pl.multiple_of(block * bucket_rows + chunk * group, group)
                rows = pl.ds(first_row, group)
                left.append((own[rows, re_cols], own[rows, im_cols]))
            for place in range(src_count):
                right = []
                for block in range(blocks):
                    rows = slice(block * window + place * part, block * window + (place + 1) * part)
                    right.append((sources[rows, :LANES], sources[rows, LANES:]))
                for owner in range(OWNERS_STEP):
                    reals, imags = [], []
                    for rank in range(CAP):
                        row = slice(owner * CAP + rank, owner * CAP + rank + 1)
                        re_sum, im_sum = None, None
                        for block in range(blocks):
                            left_re, left_im = left[block][0][row], left[block][1][row]
                            right_re, right_im = right[block]
                            re_term = left_re * right_re + left_im * right_im
                            im_term = left_re * right_im - left_im * right_re
                            re_sum = re_term if re_sum is None else re_sum + re_term
                            im_sum = im_term if im_sum is None else im_sum + im_term
                        reals.append(re_sum)
                        imags.append(im_sum)
                    at = (chunk * OWNERS_STEP + owner) * group_rows + place * rows_dest
                    rows = pl.ds(pl.multiple_of(at, rows_dest), rows_dest)
                    cross[rows, re_cols] = jnp.concatenate(reals, axis=0).astype(jnp.bfloat16)
                    cross[rows, im_cols] = jnp.concatenate(imags, axis=0).astype(jnp.bfloat16)
            return carry

        lax.fori_loop(0, rcv_count // OWNERS_STEP, cross_step, 0)

    loads[4].wait()
    scale = 1.0 / math.sqrt(blocks * HALF)
    dests = OWNERS_SEND * src_count
    steps = devices // dests

    def bucket_copy(dest):
        return pltpu.make_async_remote_copy(
            src_ref=buckets.at[dest],
            dst_ref=arrived.at[me],
            send_sem=bucket_send,
            recv_sem=bucket_recv,
            device_id=(div(dest, src_count), mod(dest, src_count)),
            device_id_type=MESH,
        )

    def owner_step(step, carry):
        first_dest = lax.rem(div(me, dests) + 1 + step, steps) * dests
        rows = pl.ds(pl.multiple_of(first_dest * rows_dest, rows_dest), dests * rows_dest)
        result = (mxu(cross[rows, :], lags[...]) * scale).astype(jnp.bfloat16)
        buckets[pl.ds(first_dest, dests)] = result.reshape(dests, rows_dest, LAGS)

        def send(index, inner):
            dest = first_dest + mod(me + index, dests)

            @pl.when(dest != me)
            def _():
                bucket_copy(dest).start()

            return inner

        lax.fori_loop(1, dests + 1, send, 0)
        return carry

    lax.fori_loop(0, steps, owner_step, 0)
    arrived[pl.ds(me, 1)] = buckets[pl.ds(me, 1)]

    others = pl.ds(0, devices - 1)
    pltpu.make_async_copy(arrived.at[others], arrived.at[others], bucket_recv).wait()
    stacked = mxu(summing[...], arrived[...].reshape(arrivals, LAGS)) * out_scale[...]
    out[...] = stacked.reshape(SEG_PER, part, LAGS)

    pltpu.make_async_copy(buckets.at[others], buckets.at[others], bucket_send).wait()
    for step in range(1, src_count):
        start_copy(step).wait_send()
        for column in range(columns):
            source_copy(step, column).wait_send()


def on_device(rcv_count, src_count, records, window_start, channel_segment, segment_row):
    tile, samples = records.shape
    blocks = samples // NFFT
    devices = rcv_count * src_count
    window = tile * src_count // 4
    part = window // src_count
    rows_dest = CAP * part
    bucket_rows = rcv_count * CAP
    columns = HALF // LANES
    segments = channel_segment.reshape(-1, LANES)
    tables = jnp.asarray(dft_tables())
    lag_rows = jnp.asarray(lag_table())
    smem = pl.BlockSpec(memory_space=pltpu.SMEM)
    vmem = pl.BlockSpec(memory_space=pltpu.VMEM)
    hbm = pl.BlockSpec(memory_space=pltpu.HBM)
    bf16, f32, i32 = jnp.bfloat16, jnp.float32, jnp.int32
    dma = pltpu.SemaphoreType.DMA
    return pl.pallas_call(
        functools.partial(kernel, rcv_count, src_count, tile, blocks),
        out_shape=jax.ShapeDtypeStruct((SEG_PER, part, LAGS), f32),
        in_specs=[smem, hbm, hbm, hbm, hbm, hbm],
        out_specs=vmem,
        scratch_shapes=[
            pltpu.SMEM(segment_row.shape, i32),
            pltpu.VMEM(segments.shape, i32),
            pltpu.VMEM(records.shape, f32),
            pltpu.VMEM(tables.shape, bf16),
            pltpu.VMEM(lag_rows.shape, bf16),
            pltpu.VMEM(segments.shape, i32),
            pltpu.VMEM((SEG_PER * part, devices * rows_dest), bf16),
            pltpu.VMEM((SEG_PER * part, LAGS), f32),
            pltpu.VMEM((8, LANES), i32),
            pltpu.VMEM((src_count - 1, 8, LANES), i32),
            pltpu.VMEM((blocks * tile, NFFT), bf16),
            pltpu.VMEM((src_count - 1, columns, blocks * window, 2 * LANES), bf16),
            pltpu.VMEM((src_count - 1, columns, blocks * window, 2 * LANES), bf16),
            pltpu.VMEM((blocks * bucket_rows, NFFT), f32),
            pltpu.VMEM((blocks * window, 2 * LANES), f32),
            pltpu.VMEM((devices * rows_dest, NFFT), bf16),
            pltpu.VMEM((devices, rows_dest, LAGS), bf16),
            pltpu.VMEM((devices, rows_dest, LAGS), bf16),
            dma((5,)),
            dma((src_count - 1,)),
            dma((src_count - 1,)),
            dma((src_count - 1, columns)),
            dma((src_count - 1, columns)),
            dma,
            dma,
        ],
        compiler_params=pltpu.CompilerParams(
            collective_id=0, has_side_effects=True, vmem_limit_bytes=62 * 1024 * 1024
        ),
    )(window_start, segment_row, segments, records, tables, lag_rows)


def solution(mesh):
    in_specs = (P(("rcv", "src"), None), P(("rcv", "src")), P(), P())
    out_specs = P("rcv", "src", None)
    return jax.shard_map(
        functools.partial(on_device, mesh.shape["rcv"], mesh.shape["src"]),
        mesh=mesh,
        in_specs=in_specs,
        out_specs=out_specs,
        check_vma=False,
    )
```

```python
import functools
import math

import jax
import jax.numpy as jnp
import ml_dtypes
import numpy as np
from jax import lax
from jax.experimental import pallas as pl
from jax.experimental.pallas import tpu as pltpu
from jax.sharding import PartitionSpec as P

NFFT = 1024
HALF = NFFT // 2
QUART = NFFT // 4
LAGS = 256
CAP = 2
SEG_PER = 4
LANES = 128
OWNERS_STEP = 4
MESH = pl.DeviceIdType.MESH
ORDER = np.concatenate([np.arange(r, HALF, 4) for r in (0, 2, 1, 3)])


def dft_tables():
    parts = []
    for r, rows in ((0, QUART), (2, QUART), (1, 2 * QUART), (3, 2 * QUART)):
        n = np.arange(rows)
        f = np.arange(r, HALF, 4)
        angles = (n[:, None] * f[None, :] % NFFT) * (2.0 * math.pi / NFFT)
        parts.append(np.concatenate([np.cos(angles), -np.sin(angles)], axis=1))
    table = np.concatenate(parts, axis=0).astype(np.float32)
    high = table.astype(ml_dtypes.bfloat16)
    low = (table - high.astype(np.float32)).astype(ml_dtypes.bfloat16)
    return np.stack([high, low])


def lag_table():
    shifts = np.arange(LAGS) - LAGS // 2
    angles = (ORDER[:, None] * shifts[None, :] % NFFT) * (2.0 * math.pi / NFFT)
    table = np.concatenate([np.cos(angles), -np.sin(angles)], axis=0)
    return table.astype(np.float32).astype(ml_dtypes.bfloat16)


def iota(shape, axis):
    return lax.broadcasted_iota(jnp.int32, shape, axis)


def onehot(mask):
    return jnp.where(mask, 1.0, 0.0).astype(jnp.bfloat16)


def mxu(a, b):
    return jnp.dot(a, b, preferred_element_type=jnp.float32)


def kernel(
    rcv_count,
    src_count,
    tile,
    blocks,
    window_start,
    segment_row_in,
    segments_in,
    records,
    tables,
    lag_rows,
    out,
    segment_row,
    segments,
    x,
    table,
    lags,
    owner_rows,
    starts_out,
    starts_in,
    white,
    sources_out,
    sources_in,
    own,
    sources,
    cross,
    buckets,
    arrived,
    load_sems,
    start_send,
    start_recv,
    source_send,
    source_recv,
    bucket_send,
    bucket_recv,
):
    rcv = lax.axis_index("rcv")
    pos = lax.axis_index("src")
    me = rcv * src_count + pos
    devices = rcv_count * src_count
    window = tile * src_count // 4
    part = window // src_count
    bucket_rows = rcv_count * CAP
    per_row = LANES // tile
    rows_dest = CAP * part

    loads = [
        pltpu.make_async_copy(records, x, load_sems.at[0]),
        pltpu.make_async_copy(tables, table, load_sems.at[1]),
        pltpu.make_async_copy(segments_in, segments, load_sems.at[2]),
        pltpu.make_async_copy(segment_row_in, segment_row, load_sems.at[3]),
        pltpu.make_async_copy(lag_rows, lags, load_sems.at[4]),
    ]
    for load in loads:
        load.start()

    barrier = pltpu.get_barrier_semaphore()

    def greet(step, carry):
        other = lax.rem(me + step, devices)
        pl.semaphore_signal(
            barrier,
            inc=1,
            device_id=(other // src_count, lax.rem(other, src_count)),
            device_id_type=MESH,
        )
        return carry

    lax.fori_loop(1, devices, greet, 0)

    starts_out[...] = jnp.full(starts_out.shape, window_start[0], jnp.int32)

    loads[0].wait()
    pl.semaphore_wait(barrier, devices - 1)

    def start_copy(step):
        other = lax.rem(pos + step, src_count)
        return pltpu.make_async_remote_copy(
            src_ref=starts_out,
            dst_ref=starts_in.at[step - 1],
            send_sem=start_send.at[step - 1],
            recv_sem=start_recv.at[step - 1],
            device_id=(rcv, other),
            device_id_type=MESH,
        )

    for step in range(1, src_count):
        start_copy(step).start()

    quarters = []
    for quarter in range(4):
        quarters.append(
            jnp.concatenate(
                [
                    x[:, block * NFFT + quarter * QUART : block * NFFT + (quarter + 1) * QUART]
                    for block in range(blocks)
                ],
                axis=0,
            )
        )
    even_a, even_b = quarters[0] + quarters[2], quarters[1] + quarters[3]
    odd = jnp.concatenate([quarters[0] - quarters[2], quarters[1] - quarters[3]], axis=1)
    inputs = [even_a + even_b, even_a - even_b, odd, odd]
    loads[1].wait()
    height = blocks * tile
    real_parts, imag_parts = [], []
    first = 0
    for values in inputs:
        depth = values.shape[1]
        high = values.astype(jnp.bfloat16)
        low = (values - high.astype(jnp.float32)).astype(jnp.bfloat16)
        both = mxu(jnp.concatenate([high, low], axis=0), table[0, first : first + depth, :])
        total = both[:height] + both[height:] + mxu(high, table[1, first : first + depth, :])
        first += depth
        real_parts.append(total[:, :LANES])
        imag_parts.append(total[:, LANES:])
    real = jnp.concatenate(real_parts, axis=1)
    imag = jnp.concatenate(imag_parts, axis=1)
    powers = real * real + imag * imag
    mean_power = jnp.mean(powers, axis=1, keepdims=True)
    factor = lax.rsqrt(powers + 0.1 * mean_power + 1e-06)
    white[...] = jnp.concatenate([real * factor, imag * factor], axis=1).astype(jnp.bfloat16)

    def source_copy(step):
        other = lax.rem(pos + step, src_count)
        return pltpu.make_async_remote_copy(
            src_ref=sources_out.at[step - 1],
            dst_ref=sources_in.at[step - 1],
            send_sem=source_send.at[step - 1],
            recv_sem=source_recv.at[step - 1],
            device_id=(rcv, other),
            device_id_type=MESH,
        )

    for step in range(1, src_count):
        other = lax.rem(pos + step, src_count)
        start_copy(src_count - step).wait_recv()
        first_position = starts_in[src_count - step - 1, 0:1, :]
        my_place = pos - jnp.where(pos < other, 0, 1)
        row_id = iota((blocks * window, LANES), 0)
        lane_id = iota((blocks * window, LANES), 1)
        asked = (first_position + row_id % window == my_place * tile + lane_id % tile) & (
            row_id // window == lane_id // tile
        )
        sources_out[step - 1] = mxu(onehot(asked), white[...]).astype(jnp.bfloat16)
        source_copy(step).start()

    loads[2].wait()
    loads[3].wait()
    all_segments = segments[...]

    def look_up(segment, rows):
        return rows + jnp.where(all_segments == segment, segment_row[segment], 0)

    stack_rows = lax.fori_loop(
        0, segment_row.shape[0], look_up, jnp.zeros(all_segments.shape, jnp.int32), unroll=8
    )
    owners = stack_rows // SEG_PER
    slots = stack_rows - owners * SEG_PER
    owner_rows[...] = owners
    lane_a, lane_b = iota((LANES, LANES), 0), iota((LANES, LANES), 1)
    earlier = onehot((lane_a // tile == lane_b // tile) & (lane_a < lane_b))

    mine = owners == rcv
    ranks = mxu(onehot(mine), earlier)
    labels = jnp.zeros((owners.shape[0], LANES), jnp.float32)
    for rank in range(CAP):
        value = jnp.where(mine & (ranks == rank), slots + 1, 0).astype(jnp.bfloat16)
        spread = onehot(
            (lane_a // tile == lane_b // rows_dest % per_row) & (lane_b // part % CAP == rank)
        )
        labels = labels + mxu(value, spread)
    arrivals = devices * rows_dest
    labels = jnp.concatenate([labels] * (arrivals // LANES), axis=1)
    row_id = iota(labels.shape, 0)
    lane_id = iota(labels.shape, 1)
    labels = jnp.sum(
        jnp.where(row_id == lane_id // (rows_dest * per_row), labels, 0.0), axis=0, keepdims=True
    )
    out_id = iota((SEG_PER * part, arrivals), 0)
    lane_id = iota((SEG_PER * part, arrivals), 1)
    chosen = (labels == (out_id // part + 1).astype(jnp.float32)) & (
        out_id % part == lane_id % part
    )
    summing = jnp.where(chosen, 1.0, 0.0)
    counts = jnp.sum(summing, axis=1, keepdims=True)
    out_scale = 1.0 / jnp.sqrt(jnp.maximum(counts, 1.0))
    summing = summing.astype(jnp.bfloat16)

    tile_owners = owner_rows[pl.ds(me // per_row, 1), :]
    bucket_id = iota((bucket_rows, LANES), 0)
    held = bucket_id // CAP == tile_owners
    tile_ranks = mxu(onehot(held), earlier)
    placed = onehot(held & (tile_ranks == (bucket_id % CAP).astype(jnp.float32)))
    fold = onehot(
        (lane_a // tile == lax.rem(me, per_row)) & (lane_a % tile == lane_b % tile)
    )
    placed = mxu(placed, fold)
    placed = jnp.concatenate([placed] * blocks, axis=0)
    placed = jnp.where(
        iota(placed.shape, 0) // bucket_rows == iota(placed.shape, 1) // tile, placed, 0.0
    ).astype(jnp.bfloat16)

    own[...] = mxu(placed, white[...])

    loads[4].wait()
    for step in range(1, src_count):
        source_copy(step).wait_recv()
    total = sources_in[0].astype(jnp.float32)
    for step in range(2, src_count):
        total = total + sources_in[step - 1].astype(jnp.float32)
    sources[...] = total

    scale = 1.0 / math.sqrt(blocks * HALF)
    steps = rcv_count // OWNERS_STEP
    group_rows = src_count * rows_dest

    def bucket_copy(owner, place):
        return pltpu.make_async_remote_copy(
            src_ref=buckets.at[owner * src_count + place],
            dst_ref=arrived.at[me],
            send_sem=bucket_send,
            recv_sem=bucket_recv,
            device_id=(owner, place),
            device_id_type=MESH,
        )

    def owner_step(step, carry):
        chunk = lax.rem(rcv // OWNERS_STEP + 1 + step, steps)

        def cross_step(index, inner):
            re_cols = pl.ds(pl.multiple_of(index * LANES, LANES), LANES)
            im_cols = pl.ds(pl.multiple_of(HALF + index * LANES, LANES), LANES)
            group = OWNERS_STEP * CAP
            left = []
            for block in range(blocks):
                first_row = pl.multiple_of(block * bucket_rows + chunk * group, group)
                rows = pl.ds(first_row, group)
                left.append((own[rows, re_cols], own[rows, im_cols]))
            for place in range(src_count):
                right = []
                for block in range(blocks):
                    rows = slice(block * window + place * part, block * window + (place + 1) * part)
                    right.append((sources[rows, re_cols], sources[rows, im_cols]))
                for owner in range(OWNERS_STEP):
                    reals, imags = [], []
                    for rank in range(CAP):
                        row = slice(owner * CAP + rank, owner * CAP + rank + 1)
                        re_sum, im_sum = None, None
                        for block in range(blocks):
                            left_re, left_im = left[block][0][row], left[block][1][row]
                            right_re, right_im = right[block]
                            re_term = left_re * right_re + left_im * right_im
                            im_term = left_re * right_im - left_im * right_re
                            re_sum = re_term if re_sum is None else re_sum + re_term
                            im_sum = im_term if im_sum is None else im_sum + im_term
                        reals.append(re_sum)
                        imags.append(im_sum)
                    at = owner * group_rows + place * rows_dest
                    rows = slice(at, at + rows_dest)
                    cross[rows, re_cols] = jnp.concatenate(reals, axis=0).astype(jnp.bfloat16)
                    cross[rows, im_cols] = jnp.concatenate(imags, axis=0).astype(jnp.bfloat16)
            return inner

        lax.fori_loop(0, HALF // LANES, cross_step, 0)
        rows = (mxu(cross[...], lags[...]) * scale).astype(jnp.bfloat16)
        dests = OWNERS_STEP * src_count
        buckets[pl.ds(chunk * dests, dests)] = rows.reshape(dests, rows_dest, LAGS)

        def send(index, inner):
            dest = chunk * dests + index

            @pl.when(dest != me)
            def _():
                bucket_copy(dest // src_count, lax.rem(dest, src_count)).start()

            return inner

        lax.fori_loop(0, dests, send, 0)
        return carry

    lax.fori_loop(0, steps, owner_step, 0)
    arrived[pl.ds(me, 1)] = buckets[pl.ds(me, 1)]

    others = pl.ds(0, devices - 1)
    pltpu.make_async_copy(arrived.at[others], arrived.at[others], bucket_recv).wait()
    stacked = mxu(summing, arrived[...].reshape(arrivals, LAGS)) * out_scale
    out[...] = stacked.reshape(SEG_PER, part, LAGS)

    pltpu.make_async_copy(buckets.at[others], buckets.at[others], bucket_send).wait()
    for step in range(1, src_count):
        start_copy(step).wait_send()
        source_copy(step).wait_send()


def on_device(rcv_count, src_count, records, window_start, channel_segment, segment_row):
    tile, samples = records.shape
    blocks = samples // NFFT
    devices = rcv_count * src_count
    window = tile * src_count // 4
    part = window // src_count
    rows_dest = CAP * part
    bucket_rows = rcv_count * CAP
    segments = channel_segment.reshape(-1, LANES)
    tables = jnp.asarray(dft_tables())
    lag_rows = jnp.asarray(lag_table())
    smem = pl.BlockSpec(memory_space=pltpu.SMEM)
    vmem = pl.BlockSpec(memory_space=pltpu.VMEM)
    hbm = pl.BlockSpec(memory_space=pltpu.HBM)
    bf16, f32, i32 = jnp.bfloat16, jnp.float32, jnp.int32
    dma = pltpu.SemaphoreType.DMA
    return pl.pallas_call(
        functools.partial(kernel, rcv_count, src_count, tile, blocks),
        out_shape=jax.ShapeDtypeStruct((SEG_PER, part, LAGS), f32),
        in_specs=[smem, hbm, hbm, hbm, hbm, hbm],
        out_specs=vmem,
        scratch_shapes=[
            pltpu.SMEM(segment_row.shape, i32),
            pltpu.VMEM(segments.shape, i32),
            pltpu.VMEM(records.shape, f32),
            pltpu.VMEM(tables.shape, bf16),
            pltpu.VMEM(lag_rows.shape, bf16),
            pltpu.VMEM(segments.shape, i32),
            pltpu.VMEM((8, LANES), i32),
            pltpu.VMEM((src_count - 1, 8, LANES), i32),
            pltpu.VMEM((blocks * tile, NFFT), bf16),
            pltpu.VMEM((src_count - 1, blocks * window, NFFT), bf16),
            pltpu.VMEM((src_count - 1, blocks * window, NFFT), bf16),
            pltpu.VMEM((blocks * bucket_rows, NFFT), f32),
            pltpu.VMEM((blocks * window, NFFT), f32),
            pltpu.VMEM((OWNERS_STEP * src_count * rows_dest, NFFT), bf16),
            pltpu.VMEM((devices, rows_dest, LAGS), bf16),
            pltpu.VMEM((devices, rows_dest, LAGS), bf16),
            dma((5,)),
            dma((src_count - 1,)),
            dma((src_count - 1,)),
            dma((src_count - 1,)),
            dma((src_count - 1,)),
            dma,
            dma,
        ],
        compiler_params=pltpu.CompilerParams(
            collective_id=0, has_side_effects=True, vmem_limit_bytes=48 * 1024 * 1024
        ),
    )(
        window_start,
        *(
            pltpu.with_memory_space_constraint(operand, pltpu.HBM)
            for operand in (segment_row, segments, records, tables, lag_rows)
        ),
    )


def solution(mesh):
    in_specs = (P(("rcv", "src"), None), P(("rcv", "src")), P(), P())
    out_specs = P("rcv", "src", None)
    return jax.shard_map(
        functools.partial(on_device, mesh.shape["rcv"], mesh.shape["src"]),
        mesh=mesh,
        in_specs=in_specs,
        out_specs=out_specs,
        check_vma=False,
    )
```

```python
import functools
import math

import jax
import jax.numpy as jnp
import ml_dtypes
import numpy as np
from jax import lax
from jax.experimental import pallas as pl
from jax.experimental.pallas import tpu as pltpu
from jax.sharding import PartitionSpec as P

NFFT = 1024
HALF = NFFT // 2
QUART = NFFT // 4
LAGS = 256
CAP = 2
SEG_PER = 4
LANES = 128
OWNERS_STEP = 4
MESH = pl.DeviceIdType.MESH
ORDER = np.concatenate([np.arange(r, HALF, 4) for r in (0, 2, 1, 3)])


def dft_tables():
    parts = []
    for r, rows in ((0, QUART), (2, QUART), (1, 2 * QUART), (3, 2 * QUART)):
        n = np.arange(rows)
        f = np.arange(r, HALF, 4)
        angles = (n[:, None] * f[None, :] % NFFT) * (2.0 * math.pi / NFFT)
        parts.append(np.concatenate([np.cos(angles), -np.sin(angles)], axis=1))
    table = np.concatenate(parts, axis=0).astype(np.float32)
    high = table.astype(ml_dtypes.bfloat16)
    low = (table - high.astype(np.float32)).astype(ml_dtypes.bfloat16)
    return np.stack([high, low])


def lag_table():
    shifts = np.arange(LAGS) - LAGS // 2
    angles = (ORDER[:, None] * shifts[None, :] % NFFT) * (2.0 * math.pi / NFFT)
    table = np.concatenate([np.cos(angles), -np.sin(angles)], axis=0)
    return table.astype(np.float32).astype(ml_dtypes.bfloat16)


def iota(shape, axis):
    return lax.broadcasted_iota(jnp.int32, shape, axis)


def div(a, b):
    return lax.shift_right_logical(a, b.bit_length() - 1) if b & (b - 1) == 0 else a // b


def mod(a, b):
    return a & (b - 1) if b & (b - 1) == 0 else a % b


def onehot(mask):
    return jnp.where(mask, 1.0, 0.0).astype(jnp.bfloat16)


def mxu(a, b):
    return jnp.dot(a, b, preferred_element_type=jnp.float32)


def kernel(
    rcv_count,
    src_count,
    tile,
    blocks,
    window_start,
    segment_row_in,
    segments_in,
    records,
    tables,
    lag_rows,
    out,
    segment_row,
    segments,
    x,
    table,
    lags,
    owner_rows,
    starts_out,
    starts_in,
    white,
    sources_out,
    sources_in,
    own,
    sources,
    cross,
    buckets,
    arrived,
    load_sems,
    start_send,
    start_recv,
    source_send,
    source_recv,
    bucket_send,
    bucket_recv,
):
    rcv = lax.axis_index("rcv")
    pos = lax.axis_index("src")
    me = rcv * src_count + pos
    devices = rcv_count * src_count
    window = tile * src_count // 4
    part = window // src_count
    bucket_rows = rcv_count * CAP
    per_row = LANES // tile
    rows_dest = CAP * part

    loads = [
        pltpu.make_async_copy(records, x, load_sems.at[0]),
        pltpu.make_async_copy(tables, table, load_sems.at[1]),
        pltpu.make_async_copy(segments_in, segments, load_sems.at[2]),
        pltpu.make_async_copy(segment_row_in, segment_row, load_sems.at[3]),
        pltpu.make_async_copy(lag_rows, lags, load_sems.at[4]),
    ]
    for load in loads:
        load.start()

    barrier = pltpu.get_barrier_semaphore()

    def greet(step, carry):
        other = lax.rem(me + step, devices)
        pl.semaphore_signal(
            barrier,
            inc=1,
            device_id=(other // src_count, lax.rem(other, src_count)),
            device_id_type=MESH,
        )
        return carry

    lax.fori_loop(1, devices, greet, 0)

    starts_out[...] = jnp.full(starts_out.shape, window_start[0], jnp.int32)

    loads[0].wait()
    pl.semaphore_wait(barrier, devices - 1)

    def start_copy(step):
        other = lax.rem(pos + step, src_count)
        return pltpu.make_async_remote_copy(
            src_ref=starts_out,
            dst_ref=starts_in.at[step - 1],
            send_sem=start_send.at[step - 1],
            recv_sem=start_recv.at[step - 1],
            device_id=(rcv, other),
            device_id_type=MESH,
        )

    for step in range(1, src_count):
        start_copy(step).start()

    quarters = []
    for quarter in range(4):
        quarters.append(
            jnp.concatenate(
                [
                    x[:, block * NFFT + quarter * QUART : block * NFFT + (quarter + 1) * QUART]
                    for block in range(blocks)
                ],
                axis=0,
            )
        )
    even_a, even_b = quarters[0] + quarters[2], quarters[1] + quarters[3]
    odd = jnp.concatenate([quarters[0] - quarters[2], quarters[1] - quarters[3]], axis=1)
    inputs = [even_a + even_b, even_a - even_b, odd, odd]
    loads[1].wait()
    height = blocks * tile
    real_parts, imag_parts = [], []
    first = 0
    for values in inputs:
        depth = values.shape[1]
        high = values.astype(jnp.bfloat16)
        low = (values - high.astype(jnp.float32)).astype(jnp.bfloat16)
        both = mxu(jnp.concatenate([high, low], axis=0), table[0, first : first + depth, :])
        total = both[:height] + both[height:] + mxu(high, table[1, first : first + depth, :])
        first += depth
        real_parts.append(total[:, :LANES])
        imag_parts.append(total[:, LANES:])
    real = jnp.concatenate(real_parts, axis=1)
    imag = jnp.concatenate(imag_parts, axis=1)
    powers = real * real + imag * imag
    mean_power = jnp.mean(powers, axis=1, keepdims=True)
    factor = lax.rsqrt(powers + 0.1 * mean_power + 1e-06)
    white[...] = jnp.concatenate([real * factor, imag * factor], axis=1).astype(jnp.bfloat16)

    def source_copy(step):
        other = lax.rem(pos + step, src_count)
        return pltpu.make_async_remote_copy(
            src_ref=sources_out.at[step - 1],
            dst_ref=sources_in.at[step - 1],
            send_sem=source_send.at[step - 1],
            recv_sem=source_recv.at[step - 1],
            device_id=(rcv, other),
            device_id_type=MESH,
        )

    row_id = iota((blocks * window, LANES), 0)
    lane_id = iota((blocks * window, LANES), 1)
    same_block = div(row_id, window) == div(lane_id, tile)
    offset = mod(row_id, window) - mod(lane_id, tile)
    for step in range(1, src_count):
        other = lax.rem(pos + step, src_count)
        start_copy(src_count - step).wait_recv()
        first_position = starts_in[src_count - step - 1, 0:1, :]
        my_place = pos - jnp.where(pos < other, 0, 1)
        asked = same_block & (offset == my_place * tile - first_position)
        sources_out[step - 1] = mxu(onehot(asked), white[...]).astype(jnp.bfloat16)
        source_copy(step).start()

    loads[2].wait()
    loads[3].wait()
    all_segments = segments[...]

    def look_up(segment, rows):
        return rows + jnp.where(all_segments == segment, segment_row[segment], 0)

    stack_rows = lax.fori_loop(
        0, segment_row.shape[0], look_up, jnp.zeros(all_segments.shape, jnp.int32), unroll=8
    )
    owners = div(stack_rows, SEG_PER)
    slots = mod(stack_rows, SEG_PER)
    owner_rows[...] = owners
    lane_a, lane_b = iota((LANES, LANES), 0), iota((LANES, LANES), 1)
    earlier = onehot((div(lane_a, tile) == div(lane_b, tile)) & (lane_a < lane_b))

    mine = owners == rcv
    ranks = mxu(onehot(mine), earlier)
    labels = jnp.zeros((owners.shape[0], LANES), jnp.float32)
    for rank in range(CAP):
        value = jnp.where(mine & (ranks == rank), slots + 1, 0).astype(jnp.bfloat16)
        spread = onehot(
            (div(lane_a, tile) == mod(div(lane_b, rows_dest), per_row))
            & (mod(div(lane_b, part), CAP) == rank)
        )
        labels = labels + mxu(value, spread)
    arrivals = devices * rows_dest
    labels = jnp.concatenate([labels] * (arrivals // LANES), axis=1)
    row_id = iota(labels.shape, 0)
    lane_id = iota(labels.shape, 1)
    labels = jnp.sum(
        jnp.where(row_id == div(lane_id, rows_dest * per_row), labels, 0.0), axis=0, keepdims=True
    )
    out_id = iota((SEG_PER * part, arrivals), 0)
    lane_id = iota((SEG_PER * part, arrivals), 1)
    chosen = (labels == (div(out_id, part) + 1).astype(jnp.float32)) & (
        mod(out_id, part) == mod(lane_id, part)
    )
    summing = jnp.where(chosen, 1.0, 0.0)
    counts = jnp.sum(summing, axis=1, keepdims=True)
    out_scale = 1.0 / jnp.sqrt(jnp.maximum(counts, 1.0))
    summing = summing.astype(jnp.bfloat16)

    tile_owners = owner_rows[pl.ds(me // per_row, 1), :]
    bucket_id = iota((bucket_rows, LANES), 0)
    held = div(bucket_id, CAP) == tile_owners
    tile_ranks = mxu(onehot(held), earlier)
    placed = onehot(held & (tile_ranks == mod(bucket_id, CAP).astype(jnp.float32)))
    fold = onehot(
        (div(lane_a, tile) == lax.rem(me, per_row)) & (mod(lane_a, tile) == mod(lane_b, tile))
    )
    placed = mxu(placed, fold)
    placed = jnp.concatenate([placed] * blocks, axis=0)
    placed = jnp.where(
        div(iota(placed.shape, 0), bucket_rows) == div(iota(placed.shape, 1), tile), placed, 0.0
    ).astype(jnp.bfloat16)

    own[...] = mxu(placed, white[...])

    loads[4].wait()
    for step in range(1, src_count):
        source_copy(step).wait_recv()
    total = sources_in[0].astype(jnp.float32)
    for step in range(2, src_count):
        total = total + sources_in[step - 1].astype(jnp.float32)
    sources[...] = total

    scale = 1.0 / math.sqrt(blocks * HALF)
    steps = rcv_count // OWNERS_STEP
    group_rows = src_count * rows_dest

    def bucket_copy(owner, place):
        return pltpu.make_async_remote_copy(
            src_ref=buckets.at[owner * src_count + place],
            dst_ref=arrived.at[me],
            send_sem=bucket_send,
            recv_sem=bucket_recv,
            device_id=(owner, place),
            device_id_type=MESH,
        )

    def owner_step(step, carry):
        chunk = lax.rem(rcv // OWNERS_STEP + 1 + step, steps)

        def cross_step(index, inner):
            re_cols = pl.ds(pl.multiple_of(index * LANES, LANES), LANES)
            im_cols = pl.ds(pl.multiple_of(HALF + index * LANES, LANES), LANES)
            group = OWNERS_STEP * CAP
            left = []
            for block in range(blocks):
                first_row = pl.multiple_of(block * bucket_rows + chunk * group, group)
                rows = pl.ds(first_row, group)
                left.append((own[rows, re_cols], own[rows, im_cols]))
            for place in range(src_count):
                right = []
                for block in range(blocks):
                    rows = slice(block * window + place * part, block * window + (place + 1) * part)
                    right.append((sources[rows, re_cols], sources[rows, im_cols]))
                for owner in range(OWNERS_STEP):
                    reals, imags = [], []
                    for rank in range(CAP):
                        row = slice(owner * CAP + rank, owner * CAP + rank + 1)
                        re_sum, im_sum = None, None
                        for block in range(blocks):
                            left_re, left_im = left[block][0][row], left[block][1][row]
                            right_re, right_im = right[block]
                            re_term = left_re * right_re + left_im * right_im
                            im_term = left_re * right_im - left_im * right_re
                            re_sum = re_term if re_sum is None else re_sum + re_term
                            im_sum = im_term if im_sum is None else im_sum + im_term
                        reals.append(re_sum)
                        imags.append(im_sum)
                    at = owner * group_rows + place * rows_dest
                    rows = slice(at, at + rows_dest)
                    cross[rows, re_cols] = jnp.concatenate(reals, axis=0).astype(jnp.bfloat16)
                    cross[rows, im_cols] = jnp.concatenate(imags, axis=0).astype(jnp.bfloat16)
            return inner

        lax.fori_loop(0, HALF // LANES, cross_step, 0)
        rows = (mxu(cross[...], lags[...]) * scale).astype(jnp.bfloat16)
        dests = OWNERS_STEP * src_count
        buckets[pl.ds(chunk * dests, dests)] = rows.reshape(dests, rows_dest, LAGS)

        def send(index, inner):
            dest = chunk * dests + index

            @pl.when(dest != me)
            def _():
                bucket_copy(dest // src_count, lax.rem(dest, src_count)).start()

            return inner

        lax.fori_loop(0, dests, send, 0)
        return carry

    lax.fori_loop(0, steps, owner_step, 0)
    arrived[pl.ds(me, 1)] = buckets[pl.ds(me, 1)]

    others = pl.ds(0, devices - 1)
    pltpu.make_async_copy(arrived.at[others], arrived.at[others], bucket_recv).wait()
    stacked = mxu(summing, arrived[...].reshape(arrivals, LAGS)) * out_scale
    out[...] = stacked.reshape(SEG_PER, part, LAGS)

    pltpu.make_async_copy(buckets.at[others], buckets.at[others], bucket_send).wait()
    for step in range(1, src_count):
        start_copy(step).wait_send()
        source_copy(step).wait_send()


def on_device(rcv_count, src_count, records, window_start, channel_segment, segment_row):
    tile, samples = records.shape
    blocks = samples // NFFT
    devices = rcv_count * src_count
    window = tile * src_count // 4
    part = window // src_count
    rows_dest = CAP * part
    bucket_rows = rcv_count * CAP
    segments = channel_segment.reshape(-1, LANES)
    tables = jnp.asarray(dft_tables())
    lag_rows = jnp.asarray(lag_table())
    smem = pl.BlockSpec(memory_space=pltpu.SMEM)
    vmem = pl.BlockSpec(memory_space=pltpu.VMEM)
    hbm = pl.BlockSpec(memory_space=pltpu.HBM)
    bf16, f32, i32 = jnp.bfloat16, jnp.float32, jnp.int32
    dma = pltpu.SemaphoreType.DMA
    return pl.pallas_call(
        functools.partial(kernel, rcv_count, src_count, tile, blocks),
        out_shape=jax.ShapeDtypeStruct((SEG_PER, part, LAGS), f32),
        in_specs=[smem, hbm, hbm, hbm, hbm, hbm],
        out_specs=vmem,
        scratch_shapes=[
            pltpu.SMEM(segment_row.shape, i32),
            pltpu.VMEM(segments.shape, i32),
            pltpu.VMEM(records.shape, f32),
            pltpu.VMEM(tables.shape, bf16),
            pltpu.VMEM(lag_rows.shape, bf16),
            pltpu.VMEM(segments.shape, i32),
            pltpu.VMEM((8, LANES), i32),
            pltpu.VMEM((src_count - 1, 8, LANES), i32),
            pltpu.VMEM((blocks * tile, NFFT), bf16),
            pltpu.VMEM((src_count - 1, blocks * window, NFFT), bf16),
            pltpu.VMEM((src_count - 1, blocks * window, NFFT), bf16),
            pltpu.VMEM((blocks * bucket_rows, NFFT), f32),
            pltpu.VMEM((blocks * window, NFFT), f32),
            pltpu.VMEM((OWNERS_STEP * src_count * rows_dest, NFFT), bf16),
            pltpu.VMEM((devices, rows_dest, LAGS), bf16),
            pltpu.VMEM((devices, rows_dest, LAGS), bf16),
            dma((5,)),
            dma((src_count - 1,)),
            dma((src_count - 1,)),
            dma((src_count - 1,)),
            dma((src_count - 1,)),
            dma,
            dma,
        ],
        compiler_params=pltpu.CompilerParams(
            collective_id=0, has_side_effects=True, vmem_limit_bytes=48 * 1024 * 1024
        ),
    )(
        window_start,
        *(
            pltpu.with_memory_space_constraint(operand, pltpu.HBM)
            for operand in (segment_row, segments, records, tables, lag_rows)
        ),
    )


def solution(mesh):
    in_specs = (P(("rcv", "src"), None), P(("rcv", "src")), P(), P())
    out_specs = P("rcv", "src", None)
    return jax.shard_map(
        functools.partial(on_device, mesh.shape["rcv"], mesh.shape["src"]),
        mesh=mesh,
        in_specs=in_specs,
        out_specs=out_specs,
        check_vma=False,
    )
```
